512 devices in a mesh: ckpt: 2 (over x_hi), ex: 8 (over y, x_lo), par: 32 (over z, core).
Axes of the slice: x: 4 (x_hi: 2, x_lo: 2; x = x_hi * 2 + x_lo), y: 4, z: 16, core: 2. Of those that a mesh axis runs over, the one named last changes fastest.
Arguments:
- example_token_inputs: bfloat16 [2, 192, 128, 8192], P('ckpt', 'ex', None, 'par'), may hold values from -6 to 6
- example_token_cotangents: bfloat16 [2, 192, 128, 8192], P('ckpt', 'ex', None, 'par'), may hold values from -6 to 6
- query_token_inputs: bfloat16 [2, 64, 128, 8192], P('ckpt', 'ex', None, 'par'), may hold values from -6 to 6
- query_token_cotangents: bfloat16 [2, 64, 128, 8192], P('ckpt', 'ex', None, 'par'), may hold values from -6 to 6
- example_token_lengths: int32 [192], P('ex'), may hold values from 16 to 128
- query_token_lengths: int32 [64], P('ex'), may hold values from 16 to 128
- adapter_down_snapshots: bfloat16 [2, 8192, 64], P('ckpt', 'par'), may hold values from -0.25 to 0.25
- adapter_up_snapshots: bfloat16 [2, 64, 8192], P('ckpt', None, 'par'), may hold values from -0.1875 to 0.1875
- down_first_moment: float32 [2, 8192, 64], P('ckpt', 'par'), may hold values from -0.3 to 0.3
- down_second_moment: float32 [2, 8192, 64], P('ckpt', 'par'), may hold values from 0.001 to 0.16
- up_first_moment: float32 [2, 64, 8192], P('ckpt', None, 'par'), may hold values from -0.3 to 0.3
- up_second_moment: float32 [2, 64, 8192], P('ckpt', None, 'par'), may hold values from 0.001 to 0.16
- snapshot_learning_rates: float32 [2], P('ckpt'), may hold values from 0.5 to 4
Outputs:
- scores: float32 [192, 64], P('ex')
The draws below stay inside these ranges and needn't reach their ends.
All inputs are finite; a program needn't handle non-finite values.
Results may differ from the reference program's by a relative error of at most 0.0003.
Values may be sent and summed in bfloat16 or wider, within the bound.
A program may use at most 64 MiB of HBM per device.

```python
import math
import jax
import jax.numpy as jnp
from jax import lax

MODEL_WIDTH = 8192
OUTPUT_FEATURES = 8192
ADAPTER_RANK = 64
SEQ = 128
SNAPSHOT_COUNT = 2
DEMOS = 192
QUERIES = 64


def shared_pattern(key, salt, width):
    return jax.random.normal(jax.random.fold_in(key, salt), (SNAPSHOT_COUNT, SEQ, width), jnp.float32)


def coherent_normal(key, shape):
    per_example = jax.random.normal(jax.random.fold_in(key, 11), (shape[0], shape[1], 1, shape[3]), jnp.float32)
    per_token = jax.random.normal(jax.random.fold_in(key, 12), shape, jnp.float32)
    return 0.7 * per_example + 0.7 * per_token


def blended(common, own):
    return jnp.clip(0.8 * common[:, None] + 0.6 * own, -6.0, 6.0)


def feature_ramp(width, ratio):
    fraction = jnp.arange(width, dtype=jnp.float32) / jnp.float32(width - 1)
    return jnp.exp((fraction - 1.0) * jnp.log(jnp.float32(ratio)))


def rising_moment(key, shape, width, ratio):
    fraction = jnp.arange(width, dtype=jnp.float32) / jnp.float32(width - 1)
    base = jnp.exp(jax.random.uniform(key, shape, jnp.float32, jnp.log(0.001), jnp.log(0.01)))
    return (base, jnp.exp(2.0 * fraction * jnp.log(jnp.float32(ratio))))


def draw_example_token_inputs(key, part):
    common = shared_pattern(key, 101, MODEL_WIDTH)
    key = jax.random.fold_in(key, 1)
    shape = (SNAPSHOT_COUNT, DEMOS, SEQ, MODEL_WIDTH)
    own = coherent_normal(key, shape)
    return blended(common, own).astype(jnp.bfloat16)


def draw_query_token_inputs(key, part):
    common = shared_pattern(key, 101, MODEL_WIDTH)
    key = jax.random.fold_in(key, 2)
    shape = (SNAPSHOT_COUNT, QUERIES, SEQ, MODEL_WIDTH)
    own = coherent_normal(key, shape)
    ramp = feature_ramp(MODEL_WIDTH, 3.0)
    return (blended(common, own) * ramp[None, None, None, :]).astype(jnp.bfloat16)


def draw_example_token_cotangents(key, part):
    common = shared_pattern(key, 102, OUTPUT_FEATURES)
    key = jax.random.fold_in(key, 3)
    shape = (SNAPSHOT_COUNT, DEMOS, SEQ, OUTPUT_FEATURES)
    own = coherent_normal(key, shape)
    return blended(common, own).astype(jnp.bfloat16)


def draw_query_token_cotangents(key, part):
    common = shared_pattern(key, 102, OUTPUT_FEATURES)
    key = jax.random.fold_in(key, 4)
    shape = (SNAPSHOT_COUNT, QUERIES, SEQ, OUTPUT_FEATURES)
    own = coherent_normal(key, shape)
    ramp = feature_ramp(OUTPUT_FEATURES, 3.0)
    return (blended(common, own) * ramp[None, None, None, :]).astype(jnp.bfloat16)


def draw_down_second_moment(key, part):
    key = jax.random.fold_in(key, 5)
    shape = (SNAPSHOT_COUNT, MODEL_WIDTH, ADAPTER_RANK)
    base, rise = rising_moment(key, shape, MODEL_WIDTH, 3.0)
    return base * rise[None, :, None]


def draw_up_second_moment(key, part):
    key = jax.random.fold_in(key, 6)
    shape = (SNAPSHOT_COUNT, ADAPTER_RANK, OUTPUT_FEATURES)
    base, rise = rising_moment(key, shape, OUTPUT_FEATURES, 3.0)
    return base * rise[None, None, :]


def place_ends(array, rng, least, high):
    longest = array.shape.index(max(array.shape))
    spots = []
    for shift in (0, 1):
        where = [jax.random.randint(jax.random.fold_in(rng, axis), (), 0, length) for axis, length in enumerate(array.shape)]
        where[longest] = (where[longest] + shift) % array.shape[longest]
        spots.append(tuple(where))
    return array.at[spots[0]].set(least).at[spots[1]].set(high)


def level_of(key, extent, split, low, high):
    factor_of = 1.0
    for axis_at, parts in split:
        draws = jax.random.uniform(jax.random.fold_in(jax.random.fold_in(key, 6), axis_at), (parts,), jnp.float32, low / len(split), high / len(split))
        factor_of = factor_of * jnp.repeat(jnp.exp(draws), extent[axis_at] // parts).reshape((-1,) + (1,) * (len(extent) - 1 - axis_at))
    return factor_of


def noise(rng, dims, deviation, reach, cuts=(), kind=jnp.bfloat16):
    entries = deviation * jax.random.normal(rng, dims, jnp.float32)
    if cuts:
        entries = entries * level_of(rng, dims, cuts, -0.22, 0.18)
    return jnp.clip(entries, -reach, reach).astype(kind)


def setup_inputs(seed: int = 0) -> dict:
    streams_of = jax.random.split(jax.random.key(seed), 14)
    return {
        "example_token_inputs": draw_example_token_inputs(jax.random.fold_in(streams_of[13], 71), 0),
        "example_token_cotangents": draw_example_token_cotangents(jax.random.fold_in(streams_of[13], 71), 0),
        "query_token_inputs": draw_query_token_inputs(jax.random.fold_in(streams_of[13], 71), 0),
        "query_token_cotangents": draw_query_token_cotangents(jax.random.fold_in(streams_of[13], 71), 0),
        "example_token_lengths": place_ends(jax.random.randint(streams_of[4], (DEMOS,), SEQ // 8, SEQ + 1), jax.random.fold_in(streams_of[4], 1), SEQ // 8, SEQ).astype(jnp.int32),
        "query_token_lengths": place_ends(jax.random.randint(streams_of[5], (QUERIES,), SEQ // 8, SEQ + 1), jax.random.fold_in(streams_of[5], 1), SEQ // 8, SEQ).astype(jnp.int32),
        "adapter_down_snapshots": noise(streams_of[6], (SNAPSHOT_COUNT, MODEL_WIDTH, ADAPTER_RANK), (MODEL_WIDTH // 16) ** -0.5, 0.25, ((0, 2), (1, 32))),
        "adapter_up_snapshots": noise(streams_of[7], (SNAPSHOT_COUNT, ADAPTER_RANK, OUTPUT_FEATURES), (ADAPTER_RANK * 16) ** -0.5, 0.1875, ((0, 2), (2, 32))),
        "down_first_moment": noise(streams_of[8], (SNAPSHOT_COUNT, MODEL_WIDTH, ADAPTER_RANK), 0.05, 0.3, ((0, 2), (1, 32)), jnp.float32),
        "down_second_moment": draw_down_second_moment(jax.random.fold_in(streams_of[13], 71), 0),
        "up_first_moment": noise(streams_of[10], (SNAPSHOT_COUNT, ADAPTER_RANK, OUTPUT_FEATURES), 0.05, 0.3, ((0, 2), (2, 32)), jnp.float32),
        "up_second_moment": draw_up_second_moment(jax.random.fold_in(streams_of[13], 71), 0),
        "snapshot_learning_rates": jnp.clip(jnp.exp(math.log(4.0) - 2.0794415 * jax.random.uniform(streams_of[12], (SNAPSHOT_COUNT,), jnp.float32) ** level_of(streams_of[12], (SNAPSHOT_COUNT,), ((0, 2),), -0.2, 0.2)), 0.5, 4.0),
    }


ADAM_ONE = 0.9
ADAM_TWO = 0.999
ADAM_EPS = 1e-08
NORM_EPS = 1e-06

def example_gradient(inputs, cotangents, length, adapter_down_weight, adapter_up_weight):
    hidden_proj = jnp.dot(inputs, adapter_down_weight, preferred_element_type=jnp.float32)
    back_proj = jnp.dot(cotangents, adapter_up_weight.T, preferred_element_type=jnp.float32)
    position = jnp.arange(SEQ, dtype=jnp.int32)
    weight = jnp.where(position < length, 1.0 / length.astype(jnp.float32), jnp.float32(0.0))
    hidden_w = (hidden_proj * weight[:, None]).astype(jnp.bfloat16)
    back_w = (back_proj * weight[:, None]).astype(jnp.bfloat16)
    grad_up = jnp.dot(hidden_w.T, cotangents, preferred_element_type=jnp.float32)
    grad_down = jnp.dot(inputs.T, back_w, preferred_element_type=jnp.float32)
    return jnp.concatenate([grad_down.reshape(-1), grad_up.reshape(-1)])

def reference(example_token_inputs, example_token_cotangents, query_token_inputs, query_token_cotangents, example_token_lengths, query_token_lengths, adapter_down_snapshots, adapter_up_snapshots, down_first_moment, down_second_moment, up_first_moment, up_second_moment, snapshot_learning_rates):
    total = jnp.zeros((DEMOS, QUERIES), jnp.float32)
    for verify_result in range(SNAPSHOT_COUNT):
        adapter_down_weight = adapter_down_snapshots[verify_result]
        adapter_up_weight = adapter_up_snapshots[verify_result]

        def query_row(items):
            return example_gradient(items[0], items[1], items[2], adapter_down_weight, adapter_up_weight).astype(jnp.bfloat16)
        query_grads = lax.map(query_row, (query_token_inputs[verify_result], query_token_cotangents[verify_result], query_token_lengths))
        query_norms = lax.optimization_barrier(jnp.sum(jnp.square(query_grads.astype(jnp.float32)), axis=1))
        first_moment = jnp.concatenate([down_first_moment[verify_result].reshape(-1), up_first_moment[verify_result].reshape(-1)])
        second_moment = jnp.concatenate([down_second_moment[verify_result].reshape(-1), up_second_moment[verify_result].reshape(-1)])

        def demo_row(items):
            gradient = example_gradient(items[0], items[1], items[2], adapter_down_weight, adapter_up_weight)
            adjusted = (ADAM_ONE * first_moment + (1.0 - ADAM_ONE) * gradient) / (jnp.sqrt(ADAM_TWO * second_moment + (1.0 - ADAM_TWO) * gradient * gradient) + ADAM_EPS)
            adjusted = adjusted.astype(jnp.bfloat16)
            products = jnp.dot(query_grads, adjusted, preferred_element_type=jnp.float32)
            return (products, jnp.sum(jnp.square(adjusted.astype(jnp.float32))))
        products, demo_norms = lax.map(demo_row, (example_token_inputs[verify_result], example_token_cotangents[verify_result], example_token_lengths))
        scale_demo = lax.rsqrt(demo_norms + NORM_EPS)
        scale_query = lax.rsqrt(query_norms + NORM_EPS)
        total = total + snapshot_learning_rates[verify_result] * products * scale_demo[:, None] * scale_query[None, :]
    return total
```

```python
import jax
import jax.numpy as jnp
from jax import lax
from jax.experimental import pallas as pl
from jax.experimental.pallas import tpu as pltpu
from jax.sharding import PartitionSpec as P

ADAM_ONE = 0.9
ADAM_TWO = 0.999
ADAM_EPS = 1e-08
NORM_EPS = 1e-06

MESH = pl.DeviceIdType.MESH
F32 = jnp.float32
BF16 = jnp.bfloat16
EXACT = lax.Precision.HIGHEST

RINGS = 16
CORES = 2
ROWS = 4
EX = 8
DEMOS = 24
QUERIES = 8
RANKS = 64
PAIR = 2 * RANKS
TOKENS = 128
FEATURES = 256
LANES = 128
Q_HALF = QUERIES * PAIR // CORES
D_HALF = DEMOS * PAIR // CORES
Q_UNIT = Q_HALF // RINGS
D_UNIT = D_HALF // RINGS
GRAIN = 32


def nt(a, b, precision=None):
    return lax.dot_general(a, b, (((1,), (1,)), ((), ())), precision=precision, preferred_element_type=F32)


def nn(a, b, precision=None):
    return lax.dot_general(a, b, (((1,), (0,)), ((), ())), precision=precision, preferred_element_type=F32)


def iota(shape, axis):
    return lax.broadcasted_iota(jnp.int32, shape, axis)


def kernel(
    xq_h, gq_h, xd_h, gd_h, ad_h, au_h, md_h, vd_h, mu_h, vu_h, qlen, dlen, rate,
    out,
    xq, gq, xd, gd, ad, au, md, vd, mu, vu,
    adt, mom, vel,
    pq, pq_in, pd, pd_in,
    rq, rq_in, rd, rd_in,
    hq, hd,
    qs, us, qall, norms,
    fin_out, fin_in, fin_mine, fin_slots, fin_part, fin_ends,
    load_sem, core_send, core_recv, z_send, z_recv, q_send, q_recv, end_send, end_recv,
):
    me = lax.axis_index("par")
    z, c = lax.div(me, CORES), lax.rem(me, CORES)
    e = lax.axis_index("ex")
    y, x = lax.div(e, 2), lax.rem(e, 2)
    ckpt = lax.axis_index("ckpt")
    other = 1 - c
    core_peer = {"par": 2 * z + other}
    up = {"ex": 2 * lax.rem(y + 1, ROWS) + x}
    down = {"ex": 2 * lax.rem(y + ROWS - 1, ROWS) + x}
    across = {"ex": 2 * y + 1 - x}
    ckpt_peer = {"ckpt": 1 - ckpt}
    far_peer = {"ckpt": 1 - ckpt, "par": 2 * z + other}

    def z_peer(k):
        return lax.rem(z + k, RINGS)

    barrier = pltpu.get_barrier_semaphore()

    def greet(k, carry):
        pl.semaphore_signal(barrier, inc=1, device_id={"par": 2 * z_peer(k) + c}, device_id_type=MESH)
        return carry

    lax.fori_loop(1, RINGS, greet, 0)
    for peer in (core_peer, up, down, across, ckpt_peer, far_peer):
        pl.semaphore_signal(barrier, inc=1, device_id=peer, device_id_type=MESH)

    loads = [
        pltpu.make_async_copy(src, dst, load_sem.at[n])
        for n, (src, dst) in enumerate(
            ((ad_h, ad), (au_h, au), (xq_h, xq), (gq_h, gq), (xd_h, xd), (gd_h, gd), (md_h, md), (vd_h, vd), (mu_h, mu), (vu_h, vu))
        )
    ]
    for load in loads:
        load.start()

    def project(count, xs, gs, to):
        def body(i, carry):
            at = pl.multiple_of(i * 2 * TOKENS, 2 * TOKENS)
            h = nt(adt[...], xs[pl.ds(at, 2 * TOKENS), :])
            k = nt(au[...], gs[pl.ds(at, 2 * TOKENS), :])
            for n in range(2):
                to[pl.ds(at + n * PAIR, RANKS), :] = h[:, n * TOKENS : (n + 1) * TOKENS]
                to[pl.ds(at + n * PAIR + RANKS, RANKS), :] = k[:, n * TOKENS : (n + 1) * TOKENS]
            return carry

        lax.fori_loop(0, count // 2, body, 0)

    loads[0].wait()
    loads[1].wait()
    adt[...] = jnp.transpose(ad[...].astype(F32)).astype(BF16)
    loads[2].wait()
    loads[3].wait()
    project(QUERIES, xq, gq, pq)
    loads[4].wait()
    loads[5].wait()
    project(DEMOS, xd, gd, pd)
    for n in (6, 7, 8, 9):
        loads[n].wait()
    mom[0:RANKS, :] = ADAM_ONE * jnp.transpose(md[...])
    vel[0:RANKS, :] = ADAM_TWO * jnp.transpose(vd[...])
    mom[RANKS:, :] = ADAM_ONE * mu[...]
    vel[RANKS:, :] = ADAM_TWO * vu[...]

    pl.semaphore_wait(barrier, RINGS - 1 + 6)

    def to_core(n, src, dst):
        return pltpu.make_async_remote_copy(src, dst, core_send.at[n], core_recv.at[n], device_id=core_peer, device_id_type=MESH)

    q_cross = to_core(0, pq.at[pl.ds(pl.multiple_of(other * Q_HALF, Q_HALF), Q_HALF)], pq_in)
    d_cross = to_core(1, pd.at[pl.ds(pl.multiple_of(other * D_HALF, D_HALF), D_HALF)], pd_in)
    q_cross.start()
    d_cross.start()

    def fold(half, own, came, send, step):
        def body(i, carry):
            at = pl.multiple_of(i * step, step)
            total = own[pl.ds(pl.multiple_of(c * half + at, step), step), :] + came[pl.ds(at, step), :]
            came[pl.ds(at, step), :] = total
            send[pl.ds(at, step), :] = total.astype(BF16)
            return carry

        lax.fori_loop(0, half // step, body, 0)

    def scatter(n, unit, send, slots):
        def body(k, carry):
            to = z_peer(k)
            pltpu.make_async_remote_copy(
                send.at[pl.ds(pl.multiple_of(to * unit, unit), unit)],
                slots.at[z],
                z_send.at[n],
                z_recv.at[n],
                device_id={"par": 2 * to + c},
                device_id_type=MESH,
            ).start()
            return carry

        lax.fori_loop(1, RINGS, body, 0)

    def spread(n, unit, ref, at):
        def body(k, carry):
            pltpu.make_async_remote_copy(
                ref.at[pl.ds(at, unit)],
                ref.at[pl.ds(at, unit)],
                z_send.at[n],
                z_recv.at[n],
                device_id={"par": 2 * z_peer(k) + c},
                device_id_type=MESH,
            ).start()
            return carry

        lax.fori_loop(1, RINGS, body, 0)

    def await_bytes(ref, sem):
        pltpu.make_async_copy(ref, ref, sem).wait()

    q_cross.wait()
    fold(Q_HALF, pq, pq_in, rq, 128)
    scatter(0, Q_UNIT, rq, rq_in)
    d_cross.wait()
    fold(D_HALF, pd, pd_in, rd, 128)

    def gather_sum(n, unit, own, slots):
        await_bytes(slots.at[pl.ds(0, RINGS - 1)], z_recv.at[n])
        total = own[pl.ds(pl.multiple_of(z * unit, unit), unit), :]

        def body(k, total):
            return total + slots[z_peer(k)].astype(F32)

        return lax.fori_loop(1, RINGS, body, total)

    def weigh(rows, length):
        position = iota((1, TOKENS), 1)
        weight = jnp.where(position < length, 1.0 / jnp.full((1, TOKENS), length, F32), 0.0)
        return (rows * weight).astype(BF16)

    q_total = gather_sum(0, Q_UNIT, pq_in, rq_in)
    q_at = pl.multiple_of(c * Q_HALF + z * Q_UNIT, Q_UNIT)
    hq[pl.ds(q_at, Q_UNIT), :] = weigh(q_total, qlen[lax.div(c * RINGS + z, PAIR // Q_UNIT)])
    spread(1, Q_UNIT, hq, q_at)
    scatter(2, D_UNIT, rd, rd_in)

    await_bytes(hq.at[pl.ds(0, (RINGS - 1) * Q_UNIT)], z_recv.at[1])
    q_half = hq.at[pl.ds(pl.multiple_of(c * Q_HALF, Q_HALF), Q_HALF)]
    q_share = to_core(2, q_half, q_half)
    q_share.start()
    q_share.wait()

    for j in range(QUERIES):
        tokens = pl.ds(j * TOKENS, TOKENS)
        down_grad = nn(hq[pl.ds(j * PAIR + RANKS, RANKS), :], xq[tokens, :])
        up_grad = nn(hq[pl.ds(j * PAIR, RANKS), :], gq[tokens, :])
        for h in range(2):
            lanes = slice(h * LANES, (h + 1) * LANES)
            qs[h, pl.ds(j, RANKS, stride=QUERIES), :] = down_grad[:, lanes]
            qs[h, pl.ds(RANKS * QUERIES + j, RANKS, stride=QUERIES), :] = up_grad[:, lanes]
    piece_rows = RANKS * QUERIES

    def q_copy(block, piece, to):
        return pltpu.make_async_remote_copy(
            qall.at[block, piece], qall.at[block, piece], q_send.at[0], q_recv.at[block, piece], device_id=to, device_id_type=MESH
        )

    for piece in range(4):
        h, part = piece // 2, piece % 2
        qall[e, piece] = qs[h, pl.ds(part * piece_rows, piece_rows), :].astype(BF16)
        for to in (up, down, across):
            q_copy(e, piece, to).start()

    d_total = gather_sum(2, D_UNIT, pd_in, rd_in)
    d_at = pl.multiple_of(c * D_HALF + z * D_UNIT, D_UNIT)
    for k in range(D_UNIT // GRAIN):
        demo = lax.div((c * RINGS + z) * (D_UNIT // GRAIN) + k, PAIR // GRAIN)
        hd[pl.ds(d_at + k * GRAIN, GRAIN), :] = weigh(d_total[k * GRAIN : (k + 1) * GRAIN], dlen[demo])
    spread(3, D_UNIT, hd, d_at)

    above = 2 * lax.rem(y + 1, ROWS) + x
    below = 2 * lax.rem(y + ROWS - 1, ROWS) + x
    beyond = 2 * lax.rem(y + 2, ROWS) + x
    side = 2 * y + 1 - x
    side_above = 2 * lax.rem(y + 1, ROWS) + 1 - x
    side_below = 2 * lax.rem(y + ROWS - 1, ROWS) + 1 - x
    side_beyond = 2 * lax.rem(y + 2, ROWS) + 1 - x

    def arrived(block, piece):
        await_bytes(qall.at[block, piece], q_recv.at[block, piece])

    for piece in range(4):
        for block in (side, above, below):
            arrived(block, piece)
        if piece < 2:
            q_copy(above, piece, down).start()
            q_copy(side, piece, up).start()
            q_copy(side, piece, down).start()
        else:
            q_copy(below, piece, up).start()
            q_copy(above, piece, across).start()
            q_copy(below, piece, across).start()
    arrived(beyond, 0)
    q_copy(beyond, 0, across).start()
    arrived(side_above, 1)
    q_copy(side_above, 1, down).start()
    arrived(side_below, 3)
    q_copy(side_below, 3, up).start()
    arrived(beyond, 2)
    q_copy(beyond, 2, across).start()

    await_bytes(hd.at[pl.ds(0, (RINGS - 1) * D_UNIT)], z_recv.at[3])
    d_half = hd.at[pl.ds(pl.multiple_of(c * D_HALF, D_HALF), D_HALF)]
    d_share = to_core(3, d_half, d_half)
    d_share.start()
    d_share.wait()

    norms[...] = jnp.zeros_like(norms)

    def update(i, carry):
        tokens = pl.ds(pl.multiple_of(i * TOKENS, TOKENS), TOKENS)
        at = pl.multiple_of(i * PAIR, PAIR)
        squares = jnp.zeros((8, LANES), F32)
        for part, first, array in ((0, RANKS, xd), (1, 0, gd)):
            grad = nn(hd[pl.ds(at + first, RANKS), :], array[tokens, :])
            rows = slice(part * RANKS, (part + 1) * RANKS)
            top = mom[rows, :] + (1.0 - ADAM_ONE) * grad
            bottom = jnp.sqrt(vel[rows, :] + (1.0 - ADAM_TWO) * grad * grad) + ADAM_EPS
            adjusted = (top / bottom).astype(BF16).astype(F32)
            for h in range(2):
                piece = adjusted[:, h * LANES : (h + 1) * LANES]
                us[h, pl.ds(part * RANKS * DEMOS + i, RANKS, stride=DEMOS), :] = piece
                squares += jnp.sum((piece * piece).reshape(RANKS // 8, 8, LANES), axis=0)
        norms[pl.ds(EX * QUERIES + i, 1), :] = jnp.sum(squares, axis=0, keepdims=True)
        return carry

    lax.fori_loop(0, DEMOS, update, 0)

    for block, pieces in ((beyond, (1, 3)), (side_above, (0, 2, 3)), (side_below, (0, 1, 2)), (side_beyond, (0, 1, 2, 3))):
        for piece in pieces:
            arrived(block, piece)

    def query_norms(n, carry):
        def body(i, total):
            rows = qall[n, lax.div(i, 8), pl.ds(pl.multiple_of(lax.rem(i, 8) * 64, 64), 64), :].astype(F32)
            return total + jnp.sum((rows * rows).reshape(8, 8, LANES), axis=0)

        total = lax.fori_loop(0, 32, body, jnp.zeros((8, LANES), F32))
        norms[pl.ds(pl.multiple_of(n * QUERIES, QUERIES), QUERIES), :] = total
        return carry

    lax.fori_loop(0, EX, query_norms, 0)

    def products(part):
        def body(r, total):
            u_at = pl.multiple_of(part * RANKS * DEMOS + r * 2 * DEMOS, 2 * DEMOS)
            q_at = pl.multiple_of(r * 2 * QUERIES, 2 * QUERIES)
            left = jnp.concatenate([us[h, pl.ds(u_at, 2 * DEMOS), :] for h in range(2)], axis=1).astype(BF16)
            right = jnp.concatenate(
                [
                    jnp.concatenate([qall[n, 2 * h + part, pl.ds(q_at, 2 * QUERIES), :] for n in range(EX)], axis=0)
                    for h in range(2)
                ],
                axis=1,
            )
            return total + nt(left, right)

        return body

    total = jnp.zeros((2 * DEMOS, 2 * EX * QUERIES), F32)
    for part in range(2):
        total = lax.fori_loop(0, RANKS // 2, products(part), total)

    second = lax.rem(lax.div(iota((DEMOS, LANES), 1), QUERIES), 2) == 1
    folded = jnp.where(second, total[DEMOS:], total[:DEMOS])
    source, target = iota((LANES, LANES), 0), lax.rem(iota((LANES, LANES), 1), EX * QUERIES)
    picks = (lax.div(source, 2 * QUERIES) == lax.div(target, QUERIES)) & (lax.rem(source, QUERIES) == lax.rem(target, QUERIES))
    twice = nn(folded, picks.astype(F32), EXACT)
    sums = nt(jnp.ones((8, LANES), F32), norms[...], EXACT)
    left_lanes = iota((8, LANES), 1) < LANES // 2
    row = iota((8, LANES), 0)

    def packed(core):
        chosen, at = iota((8, DEMOS), 0), iota((8, DEMOS), 1)
        first = ((chosen + 12 * core) == at) & (chosen < 6)
        last = ((chosen + 12 * core + 6) == at) & (chosen < 6)
        body = jnp.where(left_lanes, nn(first.astype(F32), twice, EXACT), nn(last.astype(F32), twice, EXACT))
        return jnp.where(row == 6, sums, body)

    fin_out[...] = packed(other)
    cross = to_core(4, fin_out, fin_in)
    cross.start()
    mine = packed(c)
    cross.wait()
    fin_slots[z] = mine + fin_in[...]
    spread_at = fin_slots.at[z]

    def finish(k, carry):
        pltpu.make_async_remote_copy(
            spread_at, spread_at, z_send.at[4], z_recv.at[4], device_id={"par": 2 * z_peer(k) + c}, device_id_type=MESH
        ).start()
        return carry

    lax.fori_loop(1, RINGS, finish, 0)
    await_bytes(fin_slots.at[pl.ds(0, RINGS - 1)], z_recv.at[4])
    whole = fin_slots[0]
    for n in range(1, RINGS):
        whole = whole + fin_slots[n]

    scale = lax.rsqrt(whole[6:7, :] + NORM_EPS)
    by_query = jnp.where(left_lanes, scale, pltpu.roll(jnp.broadcast_to(scale, (8, LANES)), LANES // 2, 1))
    lane = iota((8, LANES), 1)
    at = EX * QUERIES + 12 * c + row
    by_first = jnp.sum(jnp.where((lane == at) & (row < 6), scale, 0.0), axis=1, keepdims=True)
    by_last = jnp.sum(jnp.where((lane == at + 6) & (row < 6), scale, 0.0), axis=1, keepdims=True)
    scores = rate[0] * whole * jnp.where(left_lanes, by_first, by_last) * by_query
    fin_mine[...] = jnp.where(row < 6, scores, 0.0)

    ends = [
        pltpu.make_async_remote_copy(fin_mine, fin_ends.at[n], end_send.at[n], end_recv.at[n], device_id=to, device_id_type=MESH)
        for n, to in enumerate((ckpt_peer, core_peer, far_peer))
    ]
    for copy in ends:
        copy.start()
    for copy in ends:
        copy.wait()
    fin_part[c] = fin_mine[...] + fin_ends[0]
    fin_part[other] = fin_ends[1] + fin_ends[2]
    both = jnp.concatenate([fin_part[0], fin_part[1]], axis=0)
    demo, at = iota((DEMOS, 16), 0), iota((DEMOS, 16), 1)
    rows = nn((at == 8 * lax.div(demo, 12) + lax.rem(demo, 6)).astype(F32), both, EXACT)
    late = lax.rem(lax.div(iota((DEMOS, LANES // 2), 0), 6), 2) == 1
    out[...] = jnp.where(late, rows[:, LANES // 2 :], rows[:, : LANES // 2])

    await_bytes(rq.at[pl.ds(0, (RINGS - 1) * Q_UNIT)], z_send.at[0])
    await_bytes(hq.at[pl.ds(0, (RINGS - 1) * Q_UNIT)], z_send.at[1])
    await_bytes(rd.at[pl.ds(0, (RINGS - 1) * D_UNIT)], z_send.at[2])
    await_bytes(hd.at[pl.ds(0, (RINGS - 1) * D_UNIT)], z_send.at[3])
    await_bytes(fin_slots.at[pl.ds(0, RINGS - 1)], z_send.at[4])
    await_bytes(qall.at[pl.ds(0, EX - 1)], q_send.at[0])


def shards(
    example_token_inputs,
    example_token_cotangents,
    query_token_inputs,
    query_token_cotangents,
    example_token_lengths,
    query_token_lengths,
    adapter_down_snapshots,
    adapter_up_snapshots,
    down_first_moment,
    down_second_moment,
    up_first_moment,
    up_second_moment,
    snapshot_learning_rates,
):
    anywhere, scalars = pl.BlockSpec(memory_space=pl.ANY), pl.BlockSpec(memory_space=pltpu.SMEM)
    vmem = pltpu.VMEM
    dma = pltpu.SemaphoreType.DMA
    return pl.pallas_call(
        kernel,
        out_shape=jax.ShapeDtypeStruct((DEMOS, EX * QUERIES), F32),
        in_specs=[anywhere] * 10 + [scalars] * 3,
        out_specs=pl.BlockSpec(memory_space=vmem),
        scratch_shapes=[
            vmem((QUERIES * TOKENS, FEATURES), BF16),
            vmem((QUERIES * TOKENS, FEATURES), BF16),
            vmem((DEMOS * TOKENS, FEATURES), BF16),
            vmem((DEMOS * TOKENS, FEATURES), BF16),
            vmem((FEATURES, RANKS), BF16),
            vmem((RANKS, FEATURES), BF16),
            vmem((FEATURES, RANKS), F32),
            vmem((FEATURES, RANKS), F32),
            vmem((RANKS, FEATURES), F32),
            vmem((RANKS, FEATURES), F32),
            vmem((RANKS, FEATURES), BF16),
            vmem((PAIR, FEATURES), F32),
            vmem((PAIR, FEATURES), F32),
            vmem((QUERIES * PAIR, TOKENS), F32),
            vmem((Q_HALF, TOKENS), F32),
            vmem((DEMOS * PAIR, TOKENS), F32),
            vmem((D_HALF, TOKENS), F32),
            vmem((Q_HALF, TOKENS), BF16),
            vmem((RINGS, Q_UNIT, TOKENS), BF16),
            vmem((D_HALF, TOKENS), BF16),
            vmem((RINGS, D_UNIT, TOKENS), BF16),
            vmem((QUERIES * PAIR, TOKENS), BF16),
            vmem((DEMOS * PAIR, TOKENS), BF16),
            vmem((2, PAIR * QUERIES, LANES), F32),
            vmem((2, PAIR * DEMOS, LANES), F32),
            vmem((EX, 4, RANKS * QUERIES, LANES), BF16),
            vmem((LANES, LANES), F32),
            vmem((8, LANES), F32),
            vmem((8, LANES), F32),
            vmem((8, LANES), F32),
            vmem((RINGS, 8, LANES), F32),
            vmem((2, 8, LANES), F32),
            vmem((3, 8, LANES), F32),
            dma((10,)),
            dma((5,)),
            dma((5,)),
            dma((5,)),
            dma((5,)),
            dma((1,)),
            dma((EX, 4)),
            dma((3,)),
            dma((3,)),
        ],
        compiler_params=pltpu.CompilerParams(collective_id=0, has_side_effects=True, vmem_limit_bytes=40 * 2**20),
    )(
        query_token_inputs.reshape(QUERIES * TOKENS, FEATURES),
        query_token_cotangents.reshape(QUERIES * TOKENS, FEATURES),
        example_token_inputs.reshape(DEMOS * TOKENS, FEATURES),
        example_token_cotangents.reshape(DEMOS * TOKENS, FEATURES),
        adapter_down_snapshots[0],
        adapter_up_snapshots[0],
        down_first_moment[0],
        down_second_moment[0],
        up_first_moment[0],
        up_second_moment[0],
        query_token_lengths,
        example_token_lengths,
        snapshot_learning_rates,
    )


def solution(mesh):
    in_specs = (
        P("ckpt", "ex", None, "par"),
        P("ckpt", "ex", None, "par"),
        P("ckpt", "ex", None, "par"),
        P("ckpt", "ex", None, "par"),
        P("ex"),
        P("ex"),
        P("ckpt", "par", None),
        P("ckpt", None, "par"),
        P("ckpt", "par", None),
        P("ckpt", "par", None),
        P("ckpt", None, "par"),
        P("ckpt", None, "par"),
        P("ckpt"),
    )
    out_specs = P("ex", None)
    return jax.shard_map(shards, mesh=mesh, in_specs=in_specs, out_specs=out_specs, check_vma=False)
```

```python
import jax
import jax.numpy as jnp
from jax import lax
from jax.experimental import pallas as pl
from jax.experimental.pallas import tpu as pltpu
from jax.sharding import PartitionSpec as P

ADAM_ONE = 0.9
ADAM_TWO = 0.999
ADAM_EPS = 1e-08
NORM_EPS = 1e-06

MESH = pl.DeviceIdType.MESH
F32 = jnp.float32
BF16 = jnp.bfloat16
EXACT = lax.Precision.HIGHEST

RINGS = 16
CORES = 2
ROWS = 4
EX = 8
DEMOS = 24
QUERIES = 8
RANKS = 64
PAIR = 2 * RANKS
TOKENS = 128
FEATURES = 256
LANES = 128
Q_HALF = QUERIES * PAIR // CORES
D_HALF = DEMOS * PAIR // CORES
Q_UNIT = Q_HALF // RINGS
D_UNIT = D_HALF // RINGS
D_SIDE = D_UNIT // 2
D_CLASS = D_HALF // 2
CLASS = RINGS // 2
GRAIN = 16


def nt(a, b, precision=None):
    return lax.dot_general(a, b, (((1,), (1,)), ((), ())), precision=precision, preferred_element_type=F32)


def nn(a, b, precision=None):
    return lax.dot_general(a, b, (((1,), (0,)), ((), ())), precision=precision, preferred_element_type=F32)


def iota(shape, axis):
    return lax.broadcasted_iota(jnp.int32, shape, axis)


def kernel(
    xq_h, gq_h, xd_h, gd_h, ad_h, au_h, md_h, vd_h, mu_h, vu_h, qlen, dlen, rate,
    out,
    xq, gq, xd, gd, ad, au, md, vd, mu, vu,
    mom, vel,
    pq, pq_in, pd, pd_in,
    rq, rq_in, rd, rd_in, re, re_in,
    hq, hd,
    qs, us, qall, norms,
    fin_out, fin_in, fin_mine, fin_slots, fin_part, fin_ends,
    load_sem, core_send, core_recv, z_send, z_recv, q_send, q_recv, end_send, end_recv,
):
    me = lax.axis_index("par")
    z, c = lax.div(me, CORES), lax.rem(me, CORES)
    e = lax.axis_index("ex")
    y, x = lax.div(e, 2), lax.rem(e, 2)
    ckpt = lax.axis_index("ckpt")
    other = 1 - c
    core_peer = {"par": 2 * z + other}
    up = {"ex": 2 * lax.rem(y + 1, ROWS) + x}
    down = {"ex": 2 * lax.rem(y + ROWS - 1, ROWS) + x}
    across = {"ex": 2 * y + 1 - x}
    ckpt_peer = {"ckpt": 1 - ckpt}
    far_peer = {"ckpt": 1 - ckpt, "par": 2 * z + other}

    def z_peer(k):
        return lax.rem(z + k, RINGS)

    def far_first(i, count):
        return count // 2 + (2 * lax.rem(i, 2) - 1) * lax.div(i + 1, 2)

    barrier = pltpu.get_barrier_semaphore()

    def greet(k, carry):
        pl.semaphore_signal(barrier, inc=1, device_id={"par": 2 * z_peer(k) + c}, device_id_type=MESH)
        return carry

    lax.fori_loop(1, RINGS, greet, 0)
    for peer in (core_peer, up, down, across, ckpt_peer, far_peer):
        pl.semaphore_signal(barrier, inc=1, device_id=peer, device_id_type=MESH)

    loads = [
        pltpu.make_async_copy(src, dst, load_sem.at[n])
        for n, (src, dst) in enumerate(
            ((ad_h, ad), (au_h, au), (xq_h, xq), (gq_h, gq), (xd_h, xd), (gd_h, gd), (md_h, md), (vd_h, vd), (mu_h, mu), (vu_h, vu))
        )
    ]
    for load in loads:
        load.start()

    def project(count, xs, gs, to):
        def body(i, carry):
            at = pl.multiple_of(i * 2 * TOKENS, 2 * TOKENS)
            h = nt(ad[...], xs[pl.ds(at, 2 * TOKENS), :])
            k = nt(au[...], gs[pl.ds(at, 2 * TOKENS), :])
            for n in range(2):
                to[pl.ds(at + n * PAIR, RANKS), :] = h[:, n * TOKENS : (n + 1) * TOKENS]
                to[pl.ds(at + n * PAIR + RANKS, RANKS), :] = k[:, n * TOKENS : (n + 1) * TOKENS]
            return carry

        lax.fori_loop(0, count // 2, body, 0)

    loads[0].wait()
    loads[1].wait()
    loads[2].wait()
    loads[3].wait()
    project(QUERIES, xq, gq, pq)
    pl.semaphore_wait(barrier, RINGS - 1 + 6)

    def to_core(n, src, dst):
        return pltpu.make_async_remote_copy(src, dst, core_send.at[n], core_recv.at[n], device_id=core_peer, device_id_type=MESH)

    q_cross = to_core(0, pq.at[pl.ds(pl.multiple_of(other * Q_HALF, Q_HALF), Q_HALF)], pq_in)
    q_cross.start()

    def fold(half, own, came, send, step):
        def body(i, carry):
            at = pl.multiple_of(i * step, step)
            total = own[pl.ds(pl.multiple_of(c * half + at, step), step), :] + came[pl.ds(at, step), :]
            came[pl.ds(at, step), :] = total
            send[pl.ds(at, step), :] = total.astype(BF16)
            return carry

        lax.fori_loop(0, half // step, body, 0)

    def scatter(n, unit, send, slots):
        def body(i, carry):
            to = z_peer(far_first(i, RINGS))
            pltpu.make_async_remote_copy(
                send.at[pl.ds(pl.multiple_of(to * unit, unit), unit)],
                slots.at[z],
                z_send.at[n],
                z_recv.at[n],
                device_id={"par": 2 * to + c},
                device_id_type=MESH,
            ).start()
            return carry

        lax.fori_loop(0, RINGS - 1, body, 0)

    def spread(n, unit, ref, at):
        def body(i, carry):
            pltpu.make_async_remote_copy(
                ref.at[pl.ds(at, unit)],
                ref.at[pl.ds(at, unit)],
                z_send.at[n],
                z_recv.at[n],
                device_id={"par": 2 * z_peer(far_first(i, RINGS)) + c},
                device_id_type=MESH,
            ).start()
            return carry

        lax.fori_loop(0, RINGS - 1, body, 0)

    def await_bytes(ref, sem):
        pltpu.make_async_copy(ref, ref, sem).wait()

    q_cross.wait()
    fold(Q_HALF, pq, pq_in, rq, 128)
    scatter(0, Q_UNIT, rq, rq_in)
    loads[4].wait()
    loads[5].wait()
    project(DEMOS, xd, gd, pd)
    d_cross = to_core(1, pd.at[pl.ds(pl.multiple_of(other * D_HALF, D_HALF), D_HALF)], pd_in)
    d_cross.start()
    for n in (6, 7, 8, 9):
        loads[n].wait()
    mom[0:RANKS, :] = ADAM_ONE * md[...]
    vel[0:RANKS, :] = ADAM_TWO * vd[...]
    mom[RANKS:, :] = ADAM_ONE * mu[...]
    vel[RANKS:, :] = ADAM_TWO * vu[...]

    d_cross.wait()
    fold(D_HALF, pd, pd_in, rd, 128)
    parity, place = lax.rem(z, 2), lax.div(z, 2)
    sides = (lax.rem(z + 1 - 2 * parity, RINGS), lax.rem(z + RINGS - 1 + 2 * parity, RINGS))

    def to_sides(n, src, src_at, dst, dst_at):
        def body(m, carry):
            for side, to in enumerate(sides):
                at = pl.multiple_of(m * D_UNIT + side * D_SIDE, D_SIDE)
                pltpu.make_async_remote_copy(
                    src.at[pl.ds(src_at + at, D_SIDE)],
                    dst.at[pl.ds(dst_at + at, D_SIDE)],
                    z_send.at[n],
                    z_recv.at[n],
                    device_id={"par": 2 * to + c},
                    device_id_type=MESH,
                ).start()
            return carry

        lax.fori_loop(0, CLASS, body, 0)

    to_sides(2, rd, pl.multiple_of((1 - parity) * D_CLASS, D_CLASS), rd_in, 0)

    def gather_sum(n, unit, own, slots):
        await_bytes(slots.at[pl.ds(0, RINGS - 1)], z_recv.at[n])
        total = own[pl.ds(pl.multiple_of(z * unit, unit), unit), :]

        def body(k, total):
            return total + slots[z_peer(k)].astype(F32)

        return lax.fori_loop(1, RINGS, body, total)

    def weigh(rows, length):
        position = iota((1, TOKENS), 1)
        weight = jnp.where(position < length, 1.0 / jnp.full((1, TOKENS), length, F32), 0.0)
        return (rows * weight).astype(BF16)

    q_total = gather_sum(0, Q_UNIT, pq_in, rq_in)
    q_at = pl.multiple_of(c * Q_HALF + z * Q_UNIT, Q_UNIT)
    hq[pl.ds(q_at, Q_UNIT), :] = weigh(q_total, qlen[lax.div(c * RINGS + z, PAIR // Q_UNIT)])
    spread(1, Q_UNIT, hq, q_at)
    await_bytes(rd_in, z_recv.at[2])

    def fold_class(i, carry):
        at = pl.multiple_of(i * D_UNIT, D_UNIT)
        own = pl.ds(pl.multiple_of(parity * D_CLASS + at, D_UNIT), D_UNIT)
        total = pd_in[own, :] + rd_in[pl.ds(at, D_UNIT), :].astype(F32)
        pd_in[own, :] = total
        re[pl.ds(at, D_UNIT), :] = total.astype(BF16)
        return carry

    lax.fori_loop(0, CLASS, fold_class, 0)

    def class_peer(i):
        return lax.rem(place + far_first(i, CLASS), CLASS)

    def to_class(i, carry):
        m = class_peer(i)
        pltpu.make_async_remote_copy(
            re.at[pl.ds(pl.multiple_of(m * D_UNIT, D_UNIT), D_UNIT)],
            re_in.at[place],
            z_send.at[3],
            z_recv.at[3],
            device_id={"par": 2 * (2 * m + parity) + c},
            device_id_type=MESH,
        ).start()
        return carry

    lax.fori_loop(0, CLASS - 1, to_class, 0)

    await_bytes(hq.at[pl.ds(0, (RINGS - 1) * Q_UNIT)], z_recv.at[1])
    q_half = hq.at[pl.ds(pl.multiple_of(c * Q_HALF, Q_HALF), Q_HALF)]
    q_share = to_core(2, q_half, q_half)
    q_share.start()
    q_share.wait()

    for j in range(QUERIES):
        tokens = pl.ds(j * TOKENS, TOKENS)
        down_grad = nn(hq[pl.ds(j * PAIR + RANKS, RANKS), :], xq[tokens, :])
        up_grad = nn(hq[pl.ds(j * PAIR, RANKS), :], gq[tokens, :])
        for h in range(2):
            lanes = slice(h * LANES, (h + 1) * LANES)
            qs[h, pl.ds(j, RANKS, stride=QUERIES), :] = down_grad[:, lanes]
            qs[h, pl.ds(RANKS * QUERIES + j, RANKS, stride=QUERIES), :] = up_grad[:, lanes]
    piece_rows = RANKS * QUERIES

    def q_copy(block, piece, to):
        return pltpu.make_async_remote_copy(
            qall.at[block, piece], qall.at[block, piece], q_send.at[0], q_recv.at[block, piece], device_id=to, device_id_type=MESH
        )

    for piece in range(4):
        h, part = piece // 2, piece % 2
        qall[e, piece] = qs[h, pl.ds(part * piece_rows, piece_rows), :].astype(BF16)
        for to in (up, down, across):
            q_copy(e, piece, to).start()

    await_bytes(re_in.at[pl.ds(0, CLASS - 1)], z_recv.at[3])
    d_place = pl.multiple_of(parity * D_CLASS + place * D_UNIT, D_UNIT)
    d_total = lax.fori_loop(
        1, CLASS, lambda k, total: total + re_in[lax.rem(place + k, CLASS)].astype(F32), pd_in[pl.ds(d_place, D_UNIT), :]
    )
    d_at = pl.multiple_of(c * D_HALF + d_place, D_UNIT)
    for k in range(D_UNIT // GRAIN):
        demo = lax.div(lax.div(d_at, GRAIN) + k, PAIR // GRAIN)
        hd[pl.ds(d_at + k * GRAIN, GRAIN), :] = weigh(d_total[k * GRAIN : (k + 1) * GRAIN], dlen[demo])

    def spread_class(i, carry):
        ref = hd.at[pl.ds(d_at, D_UNIT)]
        to = {"par": 2 * (2 * class_peer(i) + parity) + c}
        pltpu.make_async_remote_copy(ref, ref, z_send.at[5], z_recv.at[5], device_id=to, device_id_type=MESH).start()
        return carry

    lax.fori_loop(0, CLASS - 1, spread_class, 0)

    above = 2 * lax.rem(y + 1, ROWS) + x
    below = 2 * lax.rem(y + ROWS - 1, ROWS) + x
    beyond = 2 * lax.rem(y + 2, ROWS) + x
    side = 2 * y + 1 - x
    side_above = 2 * lax.rem(y + 1, ROWS) + 1 - x
    side_below = 2 * lax.rem(y + ROWS - 1, ROWS) + 1 - x
    side_beyond = 2 * lax.rem(y + 2, ROWS) + 1 - x

    def arrived(block, piece):
        await_bytes(qall.at[block, piece], q_recv.at[block, piece])

    for piece in range(4):
        for block in (side, above, below):
            arrived(block, piece)
        if piece < 2:
            q_copy(above, piece, down).start()
            q_copy(side, piece, up).start()
            q_copy(side, piece, down).start()
        else:
            q_copy(below, piece, up).start()
            q_copy(above, piece, across).start()
            q_copy(below, piece, across).start()
    await_bytes(hd.at[pl.ds(0, (CLASS - 1) * D_UNIT)], z_recv.at[5])
    d_class = pl.multiple_of(c * D_HALF + parity * D_CLASS, D_CLASS)
    to_sides(6, hd, d_class, hd, d_class)
    arrived(beyond, 0)
    q_copy(beyond, 0, across).start()
    arrived(side_above, 1)
    q_copy(side_above, 1, down).start()
    arrived(side_below, 3)
    q_copy(side_below, 3, up).start()
    arrived(beyond, 2)
    q_copy(beyond, 2, across).start()

    norms[...] = jnp.zeros_like(norms)

    def query_norms(n, carry):
        total = jnp.zeros((8, LANES), F32)
        for piece in range(4):
            rows = qall[n, piece].astype(F32)
            total += jnp.sum((rows * rows).reshape(RANKS, QUERIES, LANES), axis=0)
        norms[pl.ds(pl.multiple_of(n * QUERIES, QUERIES), QUERIES), :] = total
        return carry

    for block in (e, side, above, below):
        query_norms(block, 0)
    await_bytes(hd.at[pl.ds(0, D_CLASS)], z_recv.at[6])
    d_half = hd.at[pl.ds(pl.multiple_of(c * D_HALF, D_HALF), D_HALF)]
    d_share = to_core(3, d_half, d_half)
    d_share.start()


    def update(i, carry):
        tokens = pl.ds(pl.multiple_of(i * TOKENS, TOKENS), TOKENS)
        at = pl.multiple_of(i * PAIR, PAIR)
        squares = jnp.zeros((8, LANES), F32)
        for part, first, array in ((0, RANKS, xd), (1, 0, gd)):
            grad = nn(hd[pl.ds(at + first, RANKS), :], array[tokens, :])
            rows = slice(part * RANKS, (part + 1) * RANKS)
            top = mom[rows, :] + (1.0 - ADAM_ONE) * grad
            bottom = jnp.sqrt(vel[rows, :] + (1.0 - ADAM_TWO) * grad * grad) + ADAM_EPS
            adjusted = (top / bottom).astype(BF16).astype(F32)
            for h in range(2):
                piece = adjusted[:, h * LANES : (h + 1) * LANES]
                us[h, pl.ds(part * RANKS * DEMOS + i, RANKS, stride=DEMOS), :] = piece
                squares += jnp.sum((piece * piece).reshape(RANKS // 8, 8, LANES), axis=0)
        norms[pl.ds(EX * QUERIES + i, 1), :] = jnp.sum(squares, axis=0, keepdims=True)
        return carry

    first = c * (DEMOS // CORES)
    lax.fori_loop(first, first + DEMOS // CORES, update, 0)
    d_share.wait()
    first = other * (DEMOS // CORES)
    lax.fori_loop(first, first + DEMOS // CORES, update, 0)

    for block, pieces in ((beyond, (1, 3)), (side_above, (0, 2, 3)), (side_below, (0, 1, 2)), (side_beyond, (0, 1, 2, 3))):
        for piece in pieces:
            arrived(block, piece)
        query_norms(block, 0)

    def products(part):
        def body(i, total):
            for n in range(8):
                r = i * 8 + n
                u_at = pl.multiple_of(part * RANKS * DEMOS + r * 2 * DEMOS, 2 * DEMOS)
                q_at = pl.multiple_of(r * 2 * QUERIES, 2 * QUERIES)
                left = jnp.concatenate([us[h, pl.ds(u_at, 2 * DEMOS), :] for h in range(2)], axis=1).astype(BF16)
                right = jnp.concatenate(
                    [
                        jnp.concatenate([qall[n, 2 * h + part, pl.ds(q_at, 2 * QUERIES), :] for n in range(EX)], axis=0)
                        for h in range(2)
                    ],
                    axis=1,
                )
                total = total + nt(left, right)
            return total

        return body

    total = jnp.zeros((2 * DEMOS, 2 * EX * QUERIES), F32)
    for part in range(2):
        total = lax.fori_loop(0, RANKS // 16, products(part), total)

    second = lax.rem(lax.div(iota((DEMOS, LANES), 1), QUERIES), 2) == 1
    folded = jnp.where(second, total[DEMOS:], total[:DEMOS])
    source, target = iota((LANES, LANES), 0), lax.rem(iota((LANES, LANES), 1), EX * QUERIES)
    picks = (lax.div(source, 2 * QUERIES) == lax.div(target, QUERIES)) & (lax.rem(source, QUERIES) == lax.rem(target, QUERIES))
    twice = nn(folded, picks.astype(F32), EXACT)
    sums = nt(jnp.ones((8, LANES), F32), norms[...], EXACT)
    left_lanes = iota((8, LANES), 1) < LANES // 2
    row = iota((8, LANES), 0)

    def packed(core):
        chosen, at = iota((8, DEMOS), 0), iota((8, DEMOS), 1)
        first = ((chosen + 12 * core) == at) & (chosen < 6)
        last = ((chosen + 12 * core + 6) == at) & (chosen < 6)
        body = jnp.where(left_lanes, nn(first.astype(F32), twice, EXACT), nn(last.astype(F32), twice, EXACT))
        return jnp.where(row == 6, sums, body)

    fin_out[...] = packed(other)
    cross = to_core(4, fin_out, fin_in)
    cross.start()
    mine = packed(c)
    cross.wait()
    fin_slots[z] = mine + fin_in[...]
    spread_at = fin_slots.at[z]

    def finish(i, carry):
        to = {"par": 2 * z_peer(far_first(i, RINGS)) + c}
        pltpu.make_async_remote_copy(spread_at, spread_at, z_send.at[4], z_recv.at[4], device_id=to, device_id_type=MESH).start()
        return carry

    lax.fori_loop(0, RINGS - 1, finish, 0)
    await_bytes(fin_slots.at[pl.ds(0, RINGS - 1)], z_recv.at[4])
    whole = fin_slots[0]
    for n in range(1, RINGS):
        whole = whole + fin_slots[n]

    scale = lax.rsqrt(whole[6:7, :] + NORM_EPS)
    by_query = jnp.where(left_lanes, scale, pltpu.roll(jnp.broadcast_to(scale, (8, LANES)), LANES // 2, 1))
    lane = iota((8, LANES), 1)
    at = EX * QUERIES + 12 * c + row
    by_first = jnp.sum(jnp.where((lane == at) & (row < 6), scale, 0.0), axis=1, keepdims=True)
    by_last = jnp.sum(jnp.where((lane == at + 6) & (row < 6), scale, 0.0), axis=1, keepdims=True)
    scores = rate[0] * whole * jnp.where(left_lanes, by_first, by_last) * by_query
    fin_mine[...] = jnp.where(row < 6, scores, 0.0)

    ends = [
        pltpu.make_async_remote_copy(fin_mine, fin_ends.at[n], end_send.at[n], end_recv.at[n], device_id=to, device_id_type=MESH)
        for n, to in enumerate((ckpt_peer, core_peer, far_peer))
    ]
    for copy in ends:
        copy.start()
    for copy in ends:
        copy.wait()
    fin_part[c] = fin_mine[...] + fin_ends[0]
    fin_part[other] = fin_ends[1] + fin_ends[2]
    both = jnp.concatenate([fin_part[0], fin_part[1]], axis=0)
    demo, at = iota((DEMOS, 16), 0), iota((DEMOS, 16), 1)
    rows = nn((at == 8 * lax.div(demo, 12) + lax.rem(demo, 6)).astype(F32), both, EXACT)
    late = lax.rem(lax.div(iota((DEMOS, LANES // 2), 0), 6), 2) == 1
    out[...] = jnp.where(late, rows[:, LANES // 2 :], rows[:, : LANES // 2])

    await_bytes(rq.at[pl.ds(0, (RINGS - 1) * Q_UNIT)], z_send.at[0])
    await_bytes(hq.at[pl.ds(0, (RINGS - 1) * Q_UNIT)], z_send.at[1])
    await_bytes(rd.at[pl.ds(0, D_CLASS)], z_send.at[2])
    await_bytes(re_in.at[pl.ds(0, CLASS - 1)], z_send.at[3])
    await_bytes(hd.at[pl.ds(0, (CLASS - 1) * D_UNIT)], z_send.at[5])
    await_bytes(hd.at[pl.ds(0, D_CLASS)], z_send.at[6])
    await_bytes(fin_slots.at[pl.ds(0, RINGS - 1)], z_send.at[4])
    await_bytes(qall.at[pl.ds(0, EX - 1)], q_send.at[0])


def shards(
    example_token_inputs,
    example_token_cotangents,
    query_token_inputs,
    query_token_cotangents,
    example_token_lengths,
    query_token_lengths,
    adapter_down_snapshots,
    adapter_up_snapshots,
    down_first_moment,
    down_second_moment,
    up_first_moment,
    up_second_moment,
    snapshot_learning_rates,
):
    anywhere, scalars = pl.BlockSpec(memory_space=pl.ANY), pl.BlockSpec(memory_space=pltpu.SMEM)
    vmem = pltpu.VMEM
    dma = pltpu.SemaphoreType.DMA
    return pl.pallas_call(
        kernel,
        out_shape=jax.ShapeDtypeStruct((DEMOS, EX * QUERIES), F32),
        in_specs=[anywhere] * 10 + [scalars] * 3,
        out_specs=pl.BlockSpec(memory_space=vmem),
        scratch_shapes=[
            vmem((QUERIES * TOKENS, FEATURES), BF16),
            vmem((QUERIES * TOKENS, FEATURES), BF16),
            vmem((DEMOS * TOKENS, FEATURES), BF16),
            vmem((DEMOS * TOKENS, FEATURES), BF16),
            vmem((RANKS, FEATURES), BF16),
            vmem((RANKS, FEATURES), BF16),
            vmem((RANKS, FEATURES), F32),
            vmem((RANKS, FEATURES), F32),
            vmem((RANKS, FEATURES), F32),
            vmem((RANKS, FEATURES), F32),
            vmem((PAIR, FEATURES), F32),
            vmem((PAIR, FEATURES), F32),
            vmem((QUERIES * PAIR, TOKENS), F32),
            vmem((Q_HALF, TOKENS), F32),
            vmem((DEMOS * PAIR, TOKENS), F32),
            vmem((D_HALF, TOKENS), F32),
            vmem((Q_HALF, TOKENS), BF16),
            vmem((RINGS, Q_UNIT, TOKENS), BF16),
            vmem((D_HALF, TOKENS), BF16),
            vmem((D_CLASS, TOKENS), BF16),
            vmem((D_CLASS, TOKENS), BF16),
            vmem((CLASS, D_UNIT, TOKENS), BF16),
            vmem((QUERIES * PAIR, TOKENS), BF16),
            vmem((DEMOS * PAIR, TOKENS), BF16),
            vmem((2, PAIR * QUERIES, LANES), F32),
            vmem((2, PAIR * DEMOS, LANES), F32),
            vmem((EX, 4, RANKS * QUERIES, LANES), BF16),
            vmem((LANES, LANES), F32),
            vmem((8, LANES), F32),
            vmem((8, LANES), F32),
            vmem((8, LANES), F32),
            vmem((RINGS, 8, LANES), F32),
            vmem((2, 8, LANES), F32),
            vmem((3, 8, LANES), F32),
            dma((10,)),
            dma((5,)),
            dma((5,)),
            dma((7,)),
            dma((7,)),
            dma((1,)),
            dma((EX, 4)),
            dma((3,)),
            dma((3,)),
        ],
        compiler_params=pltpu.CompilerParams(collective_id=0, has_side_effects=True, vmem_limit_bytes=60 * 2**20),
    )(
        query_token_inputs.reshape(QUERIES * TOKENS, FEATURES),
        query_token_cotangents.reshape(QUERIES * TOKENS, FEATURES),
        example_token_inputs.reshape(DEMOS * TOKENS, FEATURES),
        example_token_cotangents.reshape(DEMOS * TOKENS, FEATURES),
        adapter_down_snapshots[0].T,
        adapter_up_snapshots[0],
        down_first_moment[0].T,
        down_second_moment[0].T,
        up_first_moment[0],
        up_second_moment[0],
        query_token_lengths,
        example_token_lengths,
        snapshot_learning_rates,
    )


def solution(mesh):
    in_specs = (
        P("ckpt", "ex", None, "par"),
        P("ckpt", "ex", None, "par"),
        P("ckpt", "ex", None, "par"),
        P("ckpt", "ex", None, "par"),
        P("ex"),
        P("ex"),
        P("ckpt", "par", None),
        P("ckpt", None, "par"),
        P("ckpt", "par", None),
        P("ckpt", "par", None),
        P("ckpt", None, "par"),
        P("ckpt", None, "par"),
        P("ckpt"),
    )
    out_specs = P("ex", None)
    return jax.shard_map(shards, mesh=mesh, in_specs=in_specs, out_specs=out_specs, check_vma=False)
```

```python
import jax
import jax.numpy as jnp
from jax import lax
from jax.experimental import pallas as pl
from jax.experimental.pallas import tpu as pltpu
from jax.sharding import PartitionSpec as P

ADAM_ONE = 0.9
ADAM_TWO = 0.999
ADAM_EPS = 1e-08
NORM_EPS = 1e-06

MESH = pl.DeviceIdType.MESH
F32 = jnp.float32
BF16 = jnp.bfloat16
EXACT = lax.Precision.HIGHEST

RINGS = 16
CORES = 2
ROWS = 4
EX = 8
DEMOS = 24
QUERIES = 8
RANKS = 64
PAIR = 2 * RANKS
TOKENS = 128
FEATURES = 256
LANES = 128
Q_HALF = QUERIES * PAIR // CORES
D_HALF = DEMOS * PAIR // CORES
Q_PART = Q_HALF // 2
Q_UNIT = Q_PART // RINGS
D_UNIT = D_HALF // RINGS
D_SIDE = D_UNIT // 2
D_CLASS = D_HALF // 2
CLASS = RINGS // 2
GRAIN = 16


def nt(a, b, precision=None):
    return lax.dot_general(a, b, (((1,), (1,)), ((), ())), precision=precision, preferred_element_type=F32)


def nn(a, b, precision=None):
    return lax.dot_general(a, b, (((1,), (0,)), ((), ())), precision=precision, preferred_element_type=F32)


def iota(shape, axis):
    return lax.broadcasted_iota(jnp.int32, shape, axis)


def kernel(
    xq_h, gq_h, xd_h, gd_h, ad_h, au_h, md_h, vd_h, mu_h, vu_h, qlen, dlen, rate,
    out,
    xq, gq, xd, gd, ad, au, md, vd, mu, vu,
    mom, vel,
    pq, pq_in, pd, pd_in,
    rq, rq_in, rd, rd_in, re, re_in,
    hq, hd,
    qs, us, qall, norms,
    fin_out, fin_in, fin_mine, fin_slots, fin_part, fin_ends,
    load_sem, core_send, core_recv, z_send, z_recv, q_send, q_recv, end_send, end_recv,
):
    me = lax.axis_index("par")
    z, c = lax.div(me, CORES), lax.rem(me, CORES)
    e = lax.axis_index("ex")
    y, x = lax.div(e, 2), lax.rem(e, 2)
    ckpt = lax.axis_index("ckpt")
    other = 1 - c
    core_peer = {"par": 2 * z + other}
    up = {"ex": 2 * lax.rem(y + 1, ROWS) + x}
    down = {"ex": 2 * lax.rem(y + ROWS - 1, ROWS) + x}
    across = {"ex": 2 * y + 1 - x}
    ckpt_peer = {"ckpt": 1 - ckpt}
    far_peer = {"ckpt": 1 - ckpt, "par": 2 * z + other}

    def z_peer(k):
        return lax.rem(z + k, RINGS)

    def far_first(i, count):
        return count // 2 + (2 * lax.rem(i, 2) - 1) * lax.div(i + 1, 2)

    barrier = pltpu.get_barrier_semaphore()

    def greet(k, carry):
        pl.semaphore_signal(barrier, inc=1, device_id={"par": 2 * z_peer(k) + c}, device_id_type=MESH)
        return carry

    lax.fori_loop(1, RINGS, greet, 0)
    for peer in (core_peer, up, down, across, ckpt_peer, far_peer):
        pl.semaphore_signal(barrier, inc=1, device_id=peer, device_id_type=MESH)

    loads = [
        pltpu.make_async_copy(src, dst, load_sem.at[n])
        for n, (src, dst) in enumerate(
            ((ad_h, ad), (au_h, au), (xq_h, xq), (gq_h, gq), (xd_h, xd), (gd_h, gd), (md_h, md), (vd_h, vd), (mu_h, mu), (vu_h, vu))
        )
    ]
    for load in loads:
        load.start()

    def project(count, xs, gs, to, k_row, h_row):
        def body(i, carry):
            at = pl.multiple_of(i * 2 * TOKENS, 2 * TOKENS)
            h = nt(ad[...], xs[pl.ds(at, 2 * TOKENS), :])
            k = nt(au[...], gs[pl.ds(at, 2 * TOKENS), :])
            for n in range(2):
                to[pl.ds(pl.multiple_of(h_row(2 * i + n), RANKS), RANKS), :] = h[:, n * TOKENS : (n + 1) * TOKENS]
                to[pl.ds(pl.multiple_of(k_row(2 * i + n), RANKS), RANKS), :] = k[:, n * TOKENS : (n + 1) * TOKENS]
            return carry

        lax.fori_loop(0, count // 2, body, 0)

    loads[0].wait()
    loads[1].wait()
    loads[2].wait()
    loads[3].wait()


    def q_row(j, part):
        share = QUERIES // CORES
        return lax.div(j, share) * Q_HALF + part * Q_PART + lax.rem(j, share) * RANKS

    project(QUERIES, xq, gq, pq, lambda j: q_row(j, 0), lambda j: q_row(j, 1))
    loads[4].wait()
    loads[5].wait()
    project(DEMOS, xd, gd, pd, lambda j: j * PAIR + RANKS, lambda j: j * PAIR)
    for n in (6, 7, 8, 9):
        loads[n].wait()
    mom[0:RANKS, :] = ADAM_ONE * md[...]
    vel[0:RANKS, :] = ADAM_TWO * vd[...]
    mom[RANKS:, :] = ADAM_ONE * mu[...]
    vel[RANKS:, :] = ADAM_TWO * vu[...]

    pl.semaphore_wait(barrier, RINGS - 1 + 6)

    def to_core(n, src, dst):
        return pltpu.make_async_remote_copy(src, dst, core_send.at[n], core_recv.at[n], device_id=core_peer, device_id_type=MESH)

    q_cross = to_core(0, pq.at[pl.ds(pl.multiple_of(other * Q_HALF, Q_HALF), Q_HALF)], pq_in)
    d_cross = to_core(1, pd.at[pl.ds(pl.multiple_of(other * D_HALF, D_HALF), D_HALF)], pd_in)
    q_cross.start()
    d_cross.start()

    def fold(half, own, came, send, step):
        def body(i, carry):
            at = pl.multiple_of(i * step, step)
            total = own[pl.ds(pl.multiple_of(c * half + at, step), step), :] + came[pl.ds(at, step), :]
            came[pl.ds(at, step), :] = total
            send[pl.ds(at, step), :] = total.astype(BF16)
            return carry

        lax.fori_loop(0, half // step, body, 0)

    def scatter(n, part):
        def body(i, carry):
            to = z_peer(far_first(i, RINGS))
            pltpu.make_async_remote_copy(
                rq.at[pl.ds(pl.multiple_of(part * Q_PART + to * Q_UNIT, Q_UNIT), Q_UNIT)],
                rq_in.at[part, z],
                z_send.at[n],
                z_recv.at[n],
                device_id={"par": 2 * to + c},
                device_id_type=MESH,
            ).start()
            return carry

        lax.fori_loop(0, RINGS - 1, body, 0)

    def spread(n, unit, ref, at):
        def body(i, carry):
            pltpu.make_async_remote_copy(
                ref.at[pl.ds(at, unit)],
                ref.at[pl.ds(at, unit)],
                z_send.at[n],
                z_recv.at[n],
                device_id={"par": 2 * z_peer(far_first(i, RINGS)) + c},
                device_id_type=MESH,
            ).start()
            return carry

        lax.fori_loop(0, RINGS - 1, body, 0)

    def await_bytes(ref, sem):
        pltpu.make_async_copy(ref, ref, sem).wait()

    q_cross.wait()
    fold(Q_HALF, pq, pq_in, rq, 128)
    scatter(0, 0)
    scatter(1, 1)
    d_cross.wait()
    fold(D_HALF, pd, pd_in, rd, 128)
    parity, place = lax.rem(z, 2), lax.div(z, 2)
    sides = (lax.rem(z + 1 - 2 * parity, RINGS), lax.rem(z + RINGS - 1 + 2 * parity, RINGS))

    def to_side(side, n, src, src_at, dst, dst_at):
        def body(m, carry):
            at = pl.multiple_of(m * D_UNIT + side * D_SIDE, D_SIDE)
            pltpu.make_async_remote_copy(
                src.at[pl.ds(src_at + at, D_SIDE)],
                dst.at[pl.ds(dst_at + at, D_SIDE)],
                z_send.at[n],
                z_recv.at[n],
                device_id={"par": 2 * sides[side] + c},
                device_id_type=MESH,
            ).start()
            return carry

        lax.fori_loop(0, CLASS, body, 0)

    for side in range(2):
        to_side(side, 5, rd, pl.multiple_of((1 - parity) * D_CLASS, D_CLASS), rd_in, 0)
    def weigh(rows, length):
        position = iota((1, TOKENS), 1)
        weight = jnp.where(position < length, 1.0 / jnp.full((1, TOKENS), length, F32), 0.0)
        return (rows * weight).astype(BF16)

    q_length = qlen[lax.div(c * RINGS + z, RINGS * CORES // QUERIES)]
    for part in range(2):
        await_bytes(rq_in.at[part, pl.ds(0, RINGS - 1)], z_recv.at[part])
        own = pq_in[pl.ds(pl.multiple_of(part * Q_PART + z * Q_UNIT, Q_UNIT), Q_UNIT), :]
        q_total = lax.fori_loop(1, RINGS, lambda k, total, part=part: total + rq_in[part, z_peer(k)].astype(F32), own)
        q_at = pl.multiple_of(c * Q_HALF + part * Q_PART + z * Q_UNIT, Q_UNIT)
        hq[pl.ds(q_at, Q_UNIT), :] = weigh(q_total, q_length)
        spread(2 + part, Q_UNIT, hq, q_at)
    await_bytes(rd_in, z_recv.at[5])

    def fold_class(i, carry):
        at = pl.multiple_of(i * D_UNIT, D_UNIT)
        own = pl.ds(pl.multiple_of(parity * D_CLASS + at, D_UNIT), D_UNIT)
        total = pd_in[own, :] + rd_in[pl.ds(at, D_UNIT), :].astype(F32)
        pd_in[own, :] = total
        re[pl.ds(at, D_UNIT), :] = total.astype(BF16)
        return carry

    lax.fori_loop(0, CLASS, fold_class, 0)

    def class_peer(i):
        return lax.rem(place + far_first(i, CLASS), CLASS)

    def class_sums(side):
        def body(i, carry):
            m = class_peer(i)
            pltpu.make_async_remote_copy(
                re.at[pl.ds(pl.multiple_of(m * D_UNIT + side * D_SIDE, D_SIDE), D_SIDE)],
                re_in.at[side, place],
                z_send.at[6 + side],
                z_recv.at[6 + side],
                device_id={"par": 2 * (2 * m + parity) + c},
                device_id_type=MESH,
            ).start()
            return carry

        lax.fori_loop(0, CLASS - 1, body, 0)

    class_sums(0)
    class_sums(1)

    piece_rows = RANKS * QUERIES

    def q_copy(block, piece, to):
        return pltpu.make_async_remote_copy(
            qall.at[block, piece], qall.at[block, piece], q_send.at[0], q_recv.at[block, piece], device_id=to, device_id_type=MESH
        )

    for part, array in ((0, xq), (1, gq)):
        await_bytes(hq.at[pl.ds(0, (RINGS - 1) * Q_UNIT)], z_recv.at[2 + part])
        own = hq.at[pl.ds(pl.multiple_of(c * Q_HALF + part * Q_PART, Q_PART), Q_PART)]
        q_share = to_core(2 + part, own, own)
        q_share.start()
        q_share.wait()
        for j in range(QUERIES):
            at = (j // 4) * Q_HALF + part * Q_PART + (j % 4) * RANKS
            grad = nn(hq[pl.ds(at, RANKS), :], array[pl.ds(j * TOKENS, TOKENS), :])
            for h in range(2):
                qs[h, pl.ds(part * piece_rows + j, RANKS, stride=QUERIES), :] = grad[:, h * LANES : (h + 1) * LANES]
        for h in range(2):
            qall[e, 2 * part + h] = qs[h, pl.ds(part * piece_rows, piece_rows), :].astype(BF16)
            for to in (up, down, across):
                q_copy(e, 2 * part + h, to).start()

    d_class = pl.multiple_of(c * D_HALF + parity * D_CLASS, D_CLASS)

    def weigh_side(side):
        await_bytes(re_in.at[side, pl.ds(0, CLASS - 1)], z_recv.at[6 + side])
        at = pl.multiple_of(parity * D_CLASS + place * D_UNIT + side * D_SIDE, D_SIDE)
        total = lax.fori_loop(
            1, CLASS, lambda k, total: total + re_in[side, lax.rem(place + k, CLASS)].astype(F32), pd_in[pl.ds(at, D_SIDE), :]
        )
        at = pl.multiple_of(c * D_HALF + at, D_SIDE)
        for k in range(D_SIDE // GRAIN):
            demo = lax.div(lax.div(at, GRAIN) + k, PAIR // GRAIN)
            hd[pl.ds(at + k * GRAIN, GRAIN), :] = weigh(total[k * GRAIN : (k + 1) * GRAIN], dlen[demo])

        def spread_class(i, carry):
            ref = hd.at[pl.ds(at, D_SIDE)]
            to = {"par": 2 * (2 * class_peer(i) + parity) + c}
            pltpu.make_async_remote_copy(ref, ref, z_send.at[8 + side], z_recv.at[8 + side], device_id=to, device_id_type=MESH).start()
            return carry

        lax.fori_loop(0, CLASS - 1, spread_class, 0)

    def pass_side(side):
        await_bytes(hd.at[pl.ds(0, (CLASS - 1) * D_SIDE)], z_recv.at[8 + side])
        to_side(side, 10 + side, hd, d_class, hd, d_class)

    weigh_side(0)

    above = 2 * lax.rem(y + 1, ROWS) + x
    below = 2 * lax.rem(y + ROWS - 1, ROWS) + x
    beyond = 2 * lax.rem(y + 2, ROWS) + x
    side = 2 * y + 1 - x
    side_above = 2 * lax.rem(y + 1, ROWS) + 1 - x
    side_below = 2 * lax.rem(y + ROWS - 1, ROWS) + 1 - x
    side_beyond = 2 * lax.rem(y + 2, ROWS) + 1 - x

    def arrived(block, piece):
        await_bytes(qall.at[block, piece], q_recv.at[block, piece])

    for piece in range(4):
        if piece == 1:
            weigh_side(1)
        for block in (side, above, below):
            arrived(block, piece)
        if piece < 2:
            q_copy(above, piece, down).start()
            q_copy(side, piece, up).start()
            q_copy(side, piece, down).start()
        else:
            q_copy(below, piece, up).start()
            q_copy(above, piece, across).start()
            q_copy(below, piece, across).start()
    pass_side(0)
    pass_side(1)
    norms[...] = jnp.zeros_like(norms)

    def query_norms(n, carry):
        total = jnp.zeros((8, LANES), F32)
        for piece in range(4):
            rows = qall[n, piece].astype(F32)
            total += jnp.sum((rows * rows).reshape(RANKS, QUERIES, LANES), axis=0)
        norms[pl.ds(pl.multiple_of(n * QUERIES, QUERIES), QUERIES), :] = total
        return carry

    for block in (e, side, above, below):
        query_norms(block, 0)
    for side in range(2):
        await_bytes(hd.at[pl.ds(0, CLASS * D_SIDE)], z_recv.at[10 + side])
    d_half = hd.at[pl.ds(pl.multiple_of(c * D_HALF, D_HALF), D_HALF)]
    d_share = to_core(4, d_half, d_half)
    d_share.start()


    def update(i, carry):
        tokens = pl.ds(pl.multiple_of(i * TOKENS, TOKENS), TOKENS)
        at = pl.multiple_of(i * PAIR, PAIR)
        squares = jnp.zeros((8, LANES), F32)
        for part, first, array in ((0, RANKS, xd), (1, 0, gd)):
            grad = nn(hd[pl.ds(at + first, RANKS), :], array[tokens, :])
            rows = slice(part * RANKS, (part + 1) * RANKS)
            top = mom[rows, :] + (1.0 - ADAM_ONE) * grad
            bottom = jnp.sqrt(vel[rows, :] + (1.0 - ADAM_TWO) * grad * grad) + ADAM_EPS
            adjusted = (top / bottom).astype(BF16).astype(F32)
            for h in range(2):
                piece = adjusted[:, h * LANES : (h + 1) * LANES]
                us[h, pl.ds(part * RANKS * DEMOS + i, RANKS, stride=DEMOS), :] = piece
                squares += jnp.sum((piece * piece).reshape(RANKS // 8, 8, LANES), axis=0)
        norms[pl.ds(EX * QUERIES + i, 1), :] = jnp.sum(squares, axis=0, keepdims=True)
        return carry

    first = c * (DEMOS // CORES)
    lax.fori_loop(first, first + DEMOS // CORES, update, 0)
    arrived(beyond, 0)
    q_copy(beyond, 0, across).start()
    arrived(side_above, 1)
    q_copy(side_above, 1, down).start()
    arrived(side_below, 3)
    q_copy(side_below, 3, up).start()
    arrived(beyond, 2)
    q_copy(beyond, 2, across).start()

    d_share.wait()
    first = other * (DEMOS // CORES)
    lax.fori_loop(first, first + DEMOS // CORES, update, 0)

    for block, pieces in ((beyond, (1, 3)), (side_above, (0, 2, 3)), (side_below, (0, 1, 2)), (side_beyond, (0, 1, 2, 3))):
        for piece in pieces:
            arrived(block, piece)
        query_norms(block, 0)

    def products(part):
        def body(i, total):
            for n in range(8):
                r = i * 8 + n
                u_at = pl.multiple_of(part * RANKS * DEMOS + r * 2 * DEMOS, 2 * DEMOS)
                q_at = pl.multiple_of(r * 2 * QUERIES, 2 * QUERIES)
                left = jnp.concatenate([us[h, pl.ds(u_at, 2 * DEMOS), :] for h in range(2)], axis=1).astype(BF16)
                right = jnp.concatenate(
                    [
                        jnp.concatenate([qall[n, 2 * part + h, pl.ds(q_at, 2 * QUERIES), :] for n in range(EX)], axis=0)
                        for h in range(2)
                    ],
                    axis=1,
                )
                total = total + nt(left, right)
            return total

        return body

    total = jnp.zeros((2 * DEMOS, 2 * EX * QUERIES), F32)
    for part in range(2):
        total = lax.fori_loop(0, RANKS // 16, products(part), total)

    second = lax.rem(lax.div(iota((DEMOS, LANES), 1), QUERIES), 2) == 1
    folded = jnp.where(second, total[DEMOS:], total[:DEMOS])
    source, target = iota((LANES, LANES), 0), lax.rem(iota((LANES, LANES), 1), EX * QUERIES)
    picks = (lax.div(source, 2 * QUERIES) == lax.div(target, QUERIES)) & (lax.rem(source, QUERIES) == lax.rem(target, QUERIES))
    twice = nn(folded, picks.astype(F32), EXACT)
    sums = nt(jnp.ones((8, LANES), F32), norms[...], EXACT)
    left_lanes = iota((8, LANES), 1) < LANES // 2
    row = iota((8, LANES), 0)

    def packed(core):
        left, right = jnp.where(core == 0, twice[0:6], twice[12:18]), jnp.where(core == 0, twice[6:12], twice[18:24])
        body = jnp.concatenate([jnp.where(left_lanes[0:6], left, right), jnp.zeros((2, LANES), F32)], axis=0)
        return jnp.where(row == 6, sums, body)

    fin_out[...] = packed(other)
    cross = to_core(5, fin_out, fin_in)
    cross.start()
    mine = packed(c)
    cross.wait()
    fin_slots[z] = mine + fin_in[...]
    spread_at = fin_slots.at[z]

    def finish(i, carry):
        to = {"par": 2 * z_peer(far_first(i, RINGS)) + c}
        pltpu.make_async_remote_copy(spread_at, spread_at, z_send.at[4], z_recv.at[4], device_id=to, device_id_type=MESH).start()
        return carry

    lax.fori_loop(0, RINGS - 1, finish, 0)
    await_bytes(fin_slots.at[pl.ds(0, RINGS - 1)], z_recv.at[4])
    whole = fin_slots[0]
    for n in range(1, RINGS):
        whole = whole + fin_slots[n]

    scale = lax.rsqrt(whole[6:7, :] + NORM_EPS)
    by_query = jnp.where(left_lanes, scale, pltpu.roll(jnp.broadcast_to(scale, (8, LANES)), LANES // 2, 1))
    lane = iota((8, LANES), 1)
    at = EX * QUERIES + 12 * c + row
    by_first = jnp.sum(jnp.where((lane == at) & (row < 6), scale, 0.0), axis=1, keepdims=True)
    by_last = jnp.sum(jnp.where((lane == at + 6) & (row < 6), scale, 0.0), axis=1, keepdims=True)
    scores = rate[0] * whole * jnp.where(left_lanes, by_first, by_last) * by_query
    fin_mine[...] = jnp.where(row < 6, scores, 0.0)

    ends = [
        pltpu.make_async_remote_copy(fin_mine, fin_ends.at[n], end_send.at[n], end_recv.at[n], device_id=to, device_id_type=MESH)
        for n, to in enumerate((ckpt_peer, core_peer, far_peer))
    ]
    for copy in ends:
        copy.start()
    for copy in ends:
        copy.wait()
    fin_part[c] = fin_mine[...] + fin_ends[0]
    fin_part[other] = fin_ends[1] + fin_ends[2]
    rows = [fin_part[n][0:6, h * (LANES // 2) : (h + 1) * (LANES // 2)] for n in range(2) for h in range(2)]
    out[...] = jnp.concatenate(rows, axis=0)

    for n in range(4):
        await_bytes(rq.at[pl.ds(0, (RINGS - 1) * Q_UNIT)], z_send.at[n])
    await_bytes(rd.at[pl.ds(0, D_CLASS)], z_send.at[5])
    for side in range(2):
        await_bytes(re_in.at[side, pl.ds(0, CLASS - 1)], z_send.at[6 + side])
        await_bytes(hd.at[pl.ds(0, (CLASS - 1) * D_SIDE)], z_send.at[8 + side])
        await_bytes(hd.at[pl.ds(0, CLASS * D_SIDE)], z_send.at[10 + side])
    await_bytes(fin_slots.at[pl.ds(0, RINGS - 1)], z_send.at[4])
    await_bytes(qall.at[pl.ds(0, EX - 1)], q_send.at[0])


def shards(
    example_token_inputs,
    example_token_cotangents,
    query_token_inputs,
    query_token_cotangents,
    example_token_lengths,
    query_token_lengths,
    adapter_down_snapshots,
    adapter_up_snapshots,
    down_first_moment,
    down_second_moment,
    up_first_moment,
    up_second_moment,
    snapshot_learning_rates,
):
    anywhere, scalars = pl.BlockSpec(memory_space=pl.ANY), pl.BlockSpec(memory_space=pltpu.SMEM)
    vmem = pltpu.VMEM
    dma = pltpu.SemaphoreType.DMA
    return pl.pallas_call(
        kernel,
        out_shape=jax.ShapeDtypeStruct((DEMOS, EX * QUERIES), F32),
        in_specs=[anywhere] * 10 + [scalars] * 3,
        out_specs=pl.BlockSpec(memory_space=vmem),
        scratch_shapes=[
            vmem((QUERIES * TOKENS, FEATURES), BF16),
            vmem((QUERIES * TOKENS, FEATURES), BF16),
            vmem((DEMOS * TOKENS, FEATURES), BF16),
            vmem((DEMOS * TOKENS, FEATURES), BF16),
            vmem((RANKS, FEATURES), BF16),
            vmem((RANKS, FEATURES), BF16),
            vmem((RANKS, FEATURES), F32),
            vmem((RANKS, FEATURES), F32),
            vmem((RANKS, FEATURES), F32),
            vmem((RANKS, FEATURES), F32),
            vmem((PAIR, FEATURES), F32),
            vmem((PAIR, FEATURES), F32),
            vmem((QUERIES * PAIR, TOKENS), F32),
            vmem((Q_HALF, TOKENS), F32),
            vmem((DEMOS * PAIR, TOKENS), F32),
            vmem((D_HALF, TOKENS), F32),
            vmem((Q_HALF, TOKENS), BF16),
            vmem((2, RINGS, Q_UNIT, TOKENS), BF16),
            vmem((D_HALF, TOKENS), BF16),
            vmem((D_CLASS, TOKENS), BF16),
            vmem((D_CLASS, TOKENS), BF16),
            vmem((2, CLASS, D_SIDE, TOKENS), BF16),
            vmem((QUERIES * PAIR, TOKENS), BF16),
            vmem((DEMOS * PAIR, TOKENS), BF16),
            vmem((2, PAIR * QUERIES, LANES), F32),
            vmem((2, PAIR * DEMOS, LANES), F32),
            vmem((EX, 4, RANKS * QUERIES, LANES), BF16),
            vmem((LANES, LANES), F32),
            vmem((8, LANES), F32),
            vmem((8, LANES), F32),
            vmem((8, LANES), F32),
            vmem((RINGS, 8, LANES), F32),
            vmem((2, 8, LANES), F32),
            vmem((3, 8, LANES), F32),
            dma((10,)),
            dma((6,)),
            dma((6,)),
            dma((12,)),
            dma((12,)),
            dma((1,)),
            dma((EX, 4)),
            dma((3,)),
            dma((3,)),
        ],
        compiler_params=pltpu.CompilerParams(collective_id=0, has_side_effects=True, vmem_limit_bytes=60 * 2**20),
    )(
        query_token_inputs.reshape(QUERIES * TOKENS, FEATURES),
        query_token_cotangents.reshape(QUERIES * TOKENS, FEATURES),
        example_token_inputs.reshape(DEMOS * TOKENS, FEATURES),
        example_token_cotangents.reshape(DEMOS * TOKENS, FEATURES),
        adapter_down_snapshots[0].T,
        adapter_up_snapshots[0],
        down_first_moment[0].T,
        down_second_moment[0].T,
        up_first_moment[0],
        up_second_moment[0],
        query_token_lengths,
        example_token_lengths,
        snapshot_learning_rates,
    )


def solution(mesh):
    in_specs = (
        P("ckpt", "ex", None, "par"),
        P("ckpt", "ex", None, "par"),
        P("ckpt", "ex", None, "par"),
        P("ckpt", "ex", None, "par"),
        P("ex"),
        P("ex"),
        P("ckpt", "par", None),
        P("ckpt", None, "par"),
        P("ckpt", "par", None),
        P("ckpt", "par", None),
        P("ckpt", None, "par"),
        P("ckpt", None, "par"),
        P("ckpt"),
    )
    out_specs = P("ex", None)
    return jax.shard_map(shards, mesh=mesh, in_specs=in_specs, out_specs=out_specs, check_vma=False)
```

```python
import jax
import jax.numpy as jnp
from jax import lax
from jax.experimental import pallas as pl
from jax.experimental.pallas import tpu as pltpu
from jax.sharding import PartitionSpec as P

ADAM_ONE = 0.9
ADAM_TWO = 0.999
ADAM_EPS = 1e-08
NORM_EPS = 1e-06

MESH = pl.DeviceIdType.MESH
F32 = jnp.float32
BF16 = jnp.bfloat16
EXACT = lax.Precision.HIGHEST

RINGS = 16
CORES = 2
ROWS = 4
EX = 8
DEMOS = 24
QUERIES = 8
RANKS = 64
PAIR = 2 * RANKS
TOKENS = 128
FEATURES = 256
LANES = 128
Q_HALF = QUERIES * PAIR // CORES
D_HALF = DEMOS * PAIR // CORES
Q_PART = Q_HALF // 2
Q_UNIT = Q_PART // RINGS
D_UNIT = D_HALF // RINGS
D_SIDE = D_UNIT // 2
D_CLASS = D_HALF // 2
CLASS = RINGS // 2
GRAIN = 16


def nt(a, b, precision=None):
    return lax.dot_general(a, b, (((1,), (1,)), ((), ())), precision=precision, preferred_element_type=F32)


def nn(a, b, precision=None):
    return lax.dot_general(a, b, (((1,), (0,)), ((), ())), precision=precision, preferred_element_type=F32)


def iota(shape, axis):
    return lax.broadcasted_iota(jnp.int32, shape, axis)


def kernel(
    xq_h, gq_h, xd_h, gd_h, ad_h, au_h, md_h, vd_h, mu_h, vu_h, qlen, dlen, rate,
    out,
    xq, gq, xd, gd, ad, au, md, vd, mu, vu,
    mom, vel,
    pq, pq_in, pd, pd_in,
    rq, rq_in, rd, rd_in, re, re_in,
    hq, hd,
    qs, us, qall, norms, near_x, near_k,
    fin_out, fin_in, fin_mine, fin_slots, fin_part, fin_ends,
    load_sem, core_send, core_recv, z_send, z_recv, q_send, q_recv, near_send, near_recv, end_send, end_recv,
):
    me = lax.axis_index("par")
    z, c = lax.div(me, CORES), lax.rem(me, CORES)
    e = lax.axis_index("ex")
    y, x = lax.div(e, 2), lax.rem(e, 2)
    ckpt = lax.axis_index("ckpt")
    other = 1 - c
    core_peer = {"par": 2 * z + other}
    up = {"ex": 2 * lax.rem(y + 1, ROWS) + x}
    down = {"ex": 2 * lax.rem(y + ROWS - 1, ROWS) + x}
    across = {"ex": 2 * y + 1 - x}
    ckpt_peer = {"ckpt": 1 - ckpt}
    far_peer = {"ckpt": 1 - ckpt, "par": 2 * z + other}

    def z_peer(k):
        return lax.rem(z + k, RINGS)

    def far_first(i, count):
        return count // 2 + (2 * lax.rem(i, 2) - 1) * lax.div(i + 1, 2)

    barrier = pltpu.get_barrier_semaphore()

    def greet(k, carry):
        pl.semaphore_signal(barrier, inc=1, device_id={"par": 2 * z_peer(k) + c}, device_id_type=MESH)
        return carry

    lax.fori_loop(1, RINGS, greet, 0)
    for peer in (core_peer, up, down, across, ckpt_peer, far_peer):
        pl.semaphore_signal(barrier, inc=1, device_id=peer, device_id_type=MESH)

    loads = [
        pltpu.make_async_copy(src, dst, load_sem.at[n])
        for n, (src, dst) in enumerate(
            ((ad_h, ad), (au_h, au), (xq_h, xq), (gq_h, gq), (xd_h, xd), (gd_h, gd), (md_h, md), (vd_h, vd), (mu_h, mu), (vu_h, vu))
        )
    ]
    for load in loads:
        load.start()

    def project(count, xs, gs, to, k_row, h_row):
        def body(i, carry):
            at = pl.multiple_of(i * 2 * TOKENS, 2 * TOKENS)
            h = nt(ad[...], xs[pl.ds(at, 2 * TOKENS), :])
            k = nt(au[...], gs[pl.ds(at, 2 * TOKENS), :])
            for n in range(2):
                to[pl.ds(pl.multiple_of(h_row(2 * i + n), RANKS), RANKS), :] = h[:, n * TOKENS : (n + 1) * TOKENS]
                to[pl.ds(pl.multiple_of(k_row(2 * i + n), RANKS), RANKS), :] = k[:, n * TOKENS : (n + 1) * TOKENS]
            return carry

        lax.fori_loop(0, count // 2, body, 0)

    loads[0].wait()
    loads[1].wait()
    loads[2].wait()
    loads[3].wait()


    def q_row(j, part):
        share = QUERIES // CORES
        return lax.div(j, share) * Q_HALF + part * Q_PART + lax.rem(j, share) * RANKS

    project(QUERIES, xq, gq, pq, lambda j: q_row(j, 0), lambda j: q_row(j, 1))
    loads[4].wait()
    loads[5].wait()
    project(DEMOS, xd, gd, pd, lambda j: j * PAIR + RANKS, lambda j: j * PAIR)
    for n in (6, 7, 8, 9):
        loads[n].wait()
    mom[0:RANKS, :] = ADAM_ONE * md[...]
    vel[0:RANKS, :] = ADAM_TWO * vd[...]
    mom[RANKS:, :] = ADAM_ONE * mu[...]
    vel[RANKS:, :] = ADAM_TWO * vu[...]

    pl.semaphore_wait(barrier, RINGS - 1 + 6)

    def to_core(n, src, dst):
        return pltpu.make_async_remote_copy(src, dst, core_send.at[n], core_recv.at[n], device_id=core_peer, device_id_type=MESH)

    q_cross = to_core(0, pq.at[pl.ds(pl.multiple_of(other * Q_HALF, Q_HALF), Q_HALF)], pq_in)
    parity, place = lax.rem(z, 2), lax.div(z, 2)
    leaves, stays = pl.multiple_of((1 - parity) * D_CLASS, D_CLASS), pl.multiple_of(parity * D_CLASS, D_CLASS)
    d_cross = [
        to_core(n, pd.at[pl.ds(pl.multiple_of(other * D_HALF + at, D_CLASS), D_CLASS)], pd_in.at[pl.ds(at, D_CLASS)])
        for n, at in ((1, leaves), (6, stays))
    ]
    q_cross.start()

    near = ((0, across), (2, up), (1, down))

    def near_copy(n, src, dst, slot, to):
        return pltpu.make_async_remote_copy(src, dst, near_send.at[n, slot], near_recv.at[n, slot], device_id=to, device_id_type=MESH)

    x_copies = [near_copy(0, xq, near_x.at[slot], slot, to) for slot, to in near]
    for copy in x_copies:
        copy.start()
    d_cross[0].start()
    d_cross[1].start()

    def fold(count, own, own_at, came, came_at, send, send_at, step):
        def body(i, carry):
            at = pl.multiple_of(i * step, step)
            rows = pl.ds(pl.multiple_of(came_at + at, step), step)
            total = own[pl.ds(pl.multiple_of(own_at + at, step), step), :] + came[rows, :]
            came[rows, :] = total
            if send is not None:
                send[pl.ds(pl.multiple_of(send_at + at, step), step), :] = total.astype(BF16)
            return carry

        lax.fori_loop(0, count // step, body, 0)

    def scatter(n, part):
        def body(i, carry):
            to = z_peer(far_first(i, RINGS))
            pltpu.make_async_remote_copy(
                rq.at[pl.ds(pl.multiple_of(part * Q_PART + to * Q_UNIT, Q_UNIT), Q_UNIT)],
                rq_in.at[part, z],
                z_send.at[n],
                z_recv.at[n],
                device_id={"par": 2 * to + c},
                device_id_type=MESH,
            ).start()
            return carry

        lax.fori_loop(0, RINGS - 1, body, 0)

    def spread(n, unit, ref, at):
        def body(i, carry):
            pltpu.make_async_remote_copy(
                ref.at[pl.ds(at, unit)],
                ref.at[pl.ds(at, unit)],
                z_send.at[n],
                z_recv.at[n],
                device_id={"par": 2 * z_peer(far_first(i, RINGS)) + c},
                device_id_type=MESH,
            ).start()
            return carry

        lax.fori_loop(0, RINGS - 1, body, 0)

    def await_bytes(ref, sem):
        pltpu.make_async_copy(ref, ref, sem).wait()

    q_cross.wait()
    fold(Q_HALF, pq, c * Q_HALF, pq_in, 0, rq, 0, 128)
    scatter(0, 0)
    scatter(1, 1)
    d_cross[0].wait()
    fold(D_CLASS, pd, c * D_HALF + leaves, pd_in, leaves, rd, 0, 128)
    sides = (lax.rem(z + 1 - 2 * parity, RINGS), lax.rem(z + RINGS - 1 + 2 * parity, RINGS))

    def to_side(side, n, src, src_at, dst, dst_at):
        def body(m, carry):
            at = pl.multiple_of(m * D_UNIT + side * D_SIDE, D_SIDE)
            pltpu.make_async_remote_copy(
                src.at[pl.ds(src_at + at, D_SIDE)],
                dst.at[pl.ds(dst_at + at, D_SIDE)],
                z_send.at[n],
                z_recv.at[n],
                device_id={"par": 2 * sides[side] + c},
                device_id_type=MESH,
            ).start()
            return carry

        lax.fori_loop(0, CLASS, body, 0)

    for side in range(2):
        to_side(side, 5, rd, 0, rd_in, 0)
    d_cross[1].wait()
    fold(D_CLASS, pd, c * D_HALF + stays, pd_in, stays, None, 0, 128)
    def weigh(rows, length):
        position = iota((1, TOKENS), 1)
        weight = jnp.where(position < length, 1.0 / jnp.full((1, TOKENS), length, F32), 0.0)
        return (rows * weight).astype(BF16)

    def fold_class(i, carry):
        at = pl.multiple_of(i * D_UNIT, D_UNIT)
        own = pl.ds(pl.multiple_of(parity * D_CLASS + at, D_UNIT), D_UNIT)
        total = pd_in[own, :] + rd_in[pl.ds(at, D_UNIT), :].astype(F32)
        pd_in[own, :] = total
        re[pl.ds(at, D_UNIT), :] = total.astype(BF16)
        return carry

    def class_peer(i):
        return lax.rem(place + far_first(i, CLASS), CLASS)

    def class_sums(side):
        def body(i, carry):
            m = class_peer(i)
            pltpu.make_async_remote_copy(
                re.at[pl.ds(pl.multiple_of(m * D_UNIT + side * D_SIDE, D_SIDE), D_SIDE)],
                re_in.at[side, place],
                z_send.at[6 + side],
                z_recv.at[6 + side],
                device_id={"par": 2 * (2 * m + parity) + c},
                device_id_type=MESH,
            ).start()
            return carry

        lax.fori_loop(0, CLASS - 1, body, 0)

    q_length = qlen[lax.div(c * RINGS + z, RINGS * CORES // QUERIES)]
    for part in range(2):
        await_bytes(rq_in.at[part, pl.ds(0, RINGS - 1)], z_recv.at[part])
        own = pq_in[pl.ds(pl.multiple_of(part * Q_PART + z * Q_UNIT, Q_UNIT), Q_UNIT), :]
        q_total = lax.fori_loop(1, RINGS, lambda k, total, part=part: total + rq_in[part, z_peer(k)].astype(F32), own)
        q_at = pl.multiple_of(c * Q_HALF + part * Q_PART + z * Q_UNIT, Q_UNIT)
        hq[pl.ds(q_at, Q_UNIT), :] = weigh(q_total, q_length)
        spread(2 + part, Q_UNIT, hq, q_at)
    await_bytes(rd_in, z_recv.at[5])
    lax.fori_loop(0, CLASS, fold_class, 0)
    class_sums(0)
    class_sums(1)
    piece_rows = RANKS * QUERIES

    def q_copy(block, piece, to, n=0):
        return pltpu.make_async_remote_copy(
            qall.at[block, piece], qall.at[block, piece], q_send.at[n], q_recv.at[block, piece], device_id=to, device_id_type=MESH
        )

    def gradients(block, part, rows, array):
        for j in range(QUERIES):
            grad = nn(rows(j), array(j))
            for h in range(2):
                qs[h, pl.ds(part * piece_rows + j, RANKS, stride=QUERIES), :] = grad[:, h * LANES : (h + 1) * LANES]
        for h in range(2):
            qall[block, 2 * part + h] = qs[h, pl.ds(part * piece_rows, piece_rows), :].astype(BF16)

    k_copies = []
    for part, array in ((0, xq), (1, gq)):
        await_bytes(hq.at[pl.ds(0, (RINGS - 1) * Q_UNIT)], z_recv.at[2 + part])
        own = hq.at[pl.ds(pl.multiple_of(c * Q_HALF + part * Q_PART, Q_PART), Q_PART)]
        q_share = to_core(2 + part, own, own)
        q_share.start()
        q_share.wait()
        if part == 0:
            for n in range(CORES):
                for slot, to in near:
                    copy = near_copy(1 + n, hq.at[pl.ds(n * Q_HALF, Q_PART)], near_k.at[slot, pl.ds(n * Q_PART, Q_PART)], slot, to)
                    copy.start()
                    k_copies.append(copy)
        gradients(
            e,
            part,
            lambda j, part=part: hq[pl.ds((j // 4) * Q_HALF + part * Q_PART + (j % 4) * RANKS, RANKS), :],
            lambda j, array=array: array[pl.ds(j * TOKENS, TOKENS), :],
        )
        if part == 1:
            for h in range(2):
                for to in (up, down, across):
                    q_copy(e, 2 + h, to).start()

    above = 2 * lax.rem(y + 1, ROWS) + x
    below = 2 * lax.rem(y + ROWS - 1, ROWS) + x
    beyond = 2 * lax.rem(y + 2, ROWS) + x
    side = 2 * y + 1 - x
    side_above = 2 * lax.rem(y + 1, ROWS) + 1 - x
    side_below = 2 * lax.rem(y + ROWS - 1, ROWS) + 1 - x
    side_beyond = 2 * lax.rem(y + 2, ROWS) + 1 - x
    d_class = pl.multiple_of(c * D_HALF + parity * D_CLASS, D_CLASS)

    def weigh_side(side):
        await_bytes(re_in.at[side, pl.ds(0, CLASS - 1)], z_recv.at[6 + side])
        at = pl.multiple_of(parity * D_CLASS + place * D_UNIT + side * D_SIDE, D_SIDE)
        total = lax.fori_loop(
            1, CLASS, lambda k, total: total + re_in[side, lax.rem(place + k, CLASS)].astype(F32), pd_in[pl.ds(at, D_SIDE), :]
        )
        at = pl.multiple_of(c * D_HALF + at, D_SIDE)
        for k in range(D_SIDE // GRAIN):
            demo = lax.div(lax.div(at, GRAIN) + k, PAIR // GRAIN)
            hd[pl.ds(at + k * GRAIN, GRAIN), :] = weigh(total[k * GRAIN : (k + 1) * GRAIN], dlen[demo])

        def spread_class(i, carry):
            ref = hd.at[pl.ds(at, D_SIDE)]
            to = {"par": 2 * (2 * class_peer(i) + parity) + c}
            pltpu.make_async_remote_copy(ref, ref, z_send.at[8 + side], z_recv.at[8 + side], device_id=to, device_id_type=MESH).start()
            return carry

        lax.fori_loop(0, CLASS - 1, spread_class, 0)

    def pass_side(side):
        await_bytes(hd.at[pl.ds(0, (CLASS - 1) * D_SIDE)], z_recv.at[8 + side])
        to_side(side, 10 + side, hd, d_class, hd, d_class)

    weigh_side(0)
    weigh_side(1)
    for copy in x_copies + k_copies:
        copy.wait()
    for slot, block in ((1, above), (2, below), (0, side)):
        gradients(
            block,
            0,
            lambda j, slot=slot: near_k[slot, pl.ds(j * RANKS, RANKS), :],
            lambda j, slot=slot: near_x[slot, pl.ds(j * TOKENS, TOKENS), :],
        )
        if slot == 1:
            q_copy(above, 0, down).start()
            q_copy(above, 0, across).start()
        elif slot == 2:
            q_copy(below, 1, up).start()
            q_copy(below, 0, across).start()
        else:
            q_copy(side, 1, down).start()
            q_copy(side, 1, up).start()

    def arrived(block, piece):
        await_bytes(qall.at[block, piece], q_recv.at[block, piece])

    for piece in (2, 3):
        for block in (side, above, below):
            arrived(block, piece)
        if piece == 2:
            q_copy(above, 2, down, 1).start()
            q_copy(side, 2, down, 1).start()
            q_copy(side, 2, up, 1).start()
        else:
            q_copy(below, 3, up, 1).start()
            q_copy(above, 3, across, 1).start()
            q_copy(below, 3, across, 1).start()
    pass_side(0)
    pass_side(1)
    norms[...] = jnp.zeros_like(norms)

    def query_norms(n, carry):
        total = jnp.zeros((8, LANES), F32)
        for piece in range(4):
            rows = qall[n, piece].astype(F32)
            total += jnp.sum((rows * rows).reshape(RANKS, QUERIES, LANES), axis=0)
        norms[pl.ds(pl.multiple_of(n * QUERIES, QUERIES), QUERIES), :] = total
        return carry

    for block in (e, side, above, below):
        query_norms(block, 0)

    def update(i, carry):
        tokens = pl.ds(pl.multiple_of(i * TOKENS, TOKENS), TOKENS)
        at = pl.multiple_of(i * PAIR, PAIR)
        squares = jnp.zeros((8, LANES), F32)
        for part, first, array in ((0, RANKS, xd), (1, 0, gd)):
            grad = nn(hd[pl.ds(at + first, RANKS), :], array[tokens, :])
            rows = slice(part * RANKS, (part + 1) * RANKS)
            top = mom[rows, :] + (1.0 - ADAM_ONE) * grad
            bottom = jnp.sqrt(vel[rows, :] + (1.0 - ADAM_TWO) * grad * grad) + ADAM_EPS
            adjusted = (top / bottom).astype(BF16).astype(F32)
            for h in range(2):
                piece = adjusted[:, h * LANES : (h + 1) * LANES]
                us[h, pl.ds(part * RANKS * DEMOS + i, RANKS, stride=DEMOS), :] = piece
                squares += jnp.sum((piece * piece).reshape(RANKS // 8, 8, LANES), axis=0)
        norms[pl.ds(EX * QUERIES + i, 1), :] = jnp.sum(squares, axis=0, keepdims=True)
        return carry

    group = DEMOS // CORES // 2

    def update_group(core, which):
        first = core * (DEMOS // CORES) + which * group
        lax.fori_loop(first, first + group, update, 0)

    def share_class(n, which):
        ref = hd.at[pl.ds(pl.multiple_of(c * D_HALF + which * D_CLASS, D_CLASS), D_CLASS)]
        return to_core(n, ref, ref)

    share = share_class(4, parity)
    share.start()
    update_group(c, parity)
    share.wait()
    update_group(other, parity)
    arrived(side_above, 0)
    q_copy(side_above, 0, down, 1).start()
    arrived(side_below, 1)
    q_copy(side_below, 1, up, 1).start()
    arrived(beyond, 2)
    q_copy(beyond, 2, across, 1).start()
    arrived(beyond, 3)
    q_copy(beyond, 3, across, 1).start()
    for side in range(2):
        await_bytes(hd.at[pl.ds(0, CLASS * D_SIDE)], z_recv.at[10 + side])
    share = share_class(7, 1 - parity)
    share.start()
    update_group(c, 1 - parity)
    share.wait()
    update_group(other, 1 - parity)
    for block, pieces in ((beyond, (0, 1)), (side_above, (1, 2, 3)), (side_below, (0, 2, 3)), (side_beyond, (0, 1, 2, 3))):
        for piece in pieces:
            arrived(block, piece)
        query_norms(block, 0)

    def products(part):
        def body(i, total):
            for n in range(8):
                r = i * 8 + n
                u_at = pl.multiple_of(part * RANKS * DEMOS + r * 2 * DEMOS, 2 * DEMOS)
                q_at = pl.multiple_of(r * 2 * QUERIES, 2 * QUERIES)
                left = jnp.concatenate([us[h, pl.ds(u_at, 2 * DEMOS), :] for h in range(2)], axis=1).astype(BF16)
                right = jnp.concatenate(
                    [
                        jnp.concatenate([qall[n, 2 * part + h, pl.ds(q_at, 2 * QUERIES), :] for n in range(EX)], axis=0)
                        for h in range(2)
                    ],
                    axis=1,
                )
                total = total + nt(left, right)
            return total

        return body

    total = jnp.zeros((2 * DEMOS, 2 * EX * QUERIES), F32)
    for part in range(2):
        total = lax.fori_loop(0, RANKS // 16, products(part), total)

    second = lax.rem(lax.div(iota((DEMOS, LANES), 1), QUERIES), 2) == 1
    folded = jnp.where(second, total[DEMOS:], total[:DEMOS])
    source, target = iota((LANES, LANES), 0), lax.rem(iota((LANES, LANES), 1), EX * QUERIES)
    picks = (lax.div(source, 2 * QUERIES) == lax.div(target, QUERIES)) & (lax.rem(source, QUERIES) == lax.rem(target, QUERIES))
    twice = nn(folded, picks.astype(F32), EXACT)
    sums = nt(jnp.ones((8, LANES), F32), norms[...], EXACT)
    left_lanes = iota((8, LANES), 1) < LANES // 2
    row = iota((8, LANES), 0)

    def packed(core):
        left, right = jnp.where(core == 0, twice[0:6], twice[12:18]), jnp.where(core == 0, twice[6:12], twice[18:24])
        body = jnp.concatenate([jnp.where(left_lanes[0:6], left, right), jnp.zeros((2, LANES), F32)], axis=0)
        return jnp.where(row == 6, sums, body)

    fin_out[...] = packed(other)
    cross = to_core(5, fin_out, fin_in)
    cross.start()
    mine = packed(c)
    cross.wait()
    fin_slots[z] = mine + fin_in[...]
    spread_at = fin_slots.at[z]

    def finish(i, carry):
        to = {"par": 2 * z_peer(far_first(i, RINGS)) + c}
        pltpu.make_async_remote_copy(spread_at, spread_at, z_send.at[4], z_recv.at[4], device_id=to, device_id_type=MESH).start()
        return carry

    lax.fori_loop(0, RINGS - 1, finish, 0)
    await_bytes(fin_slots.at[pl.ds(0, RINGS - 1)], z_recv.at[4])
    whole = fin_slots[0]
    for n in range(1, RINGS):
        whole = whole + fin_slots[n]

    scale = lax.rsqrt(whole[6:7, :] + NORM_EPS)
    by_query = jnp.where(left_lanes, scale, pltpu.roll(jnp.broadcast_to(scale, (8, LANES)), LANES // 2, 1))
    lane = iota((8, LANES), 1)
    at = EX * QUERIES + 12 * c + row
    by_first = jnp.sum(jnp.where((lane == at) & (row < 6), scale, 0.0), axis=1, keepdims=True)
    by_last = jnp.sum(jnp.where((lane == at + 6) & (row < 6), scale, 0.0), axis=1, keepdims=True)
    scores = rate[0] * whole * jnp.where(left_lanes, by_first, by_last) * by_query
    fin_mine[...] = jnp.where(row < 6, scores, 0.0)

    ends = [
        pltpu.make_async_remote_copy(fin_mine, fin_ends.at[n], end_send.at[n], end_recv.at[n], device_id=to, device_id_type=MESH)
        for n, to in enumerate((ckpt_peer, core_peer, far_peer))
    ]
    for copy in ends:
        copy.start()
    for copy in ends:
        copy.wait()
    fin_part[c] = fin_mine[...] + fin_ends[0]
    fin_part[other] = fin_ends[1] + fin_ends[2]
    rows = [fin_part[n][0:6, h * (LANES // 2) : (h + 1) * (LANES // 2)] for n in range(2) for h in range(2)]
    out[...] = jnp.concatenate(rows, axis=0)

    for n in range(4):
        await_bytes(rq.at[pl.ds(0, (RINGS - 1) * Q_UNIT)], z_send.at[n])
    await_bytes(rd.at[pl.ds(0, D_CLASS)], z_send.at[5])
    for side in range(2):
        await_bytes(re_in.at[side, pl.ds(0, CLASS - 1)], z_send.at[6 + side])
        await_bytes(hd.at[pl.ds(0, (CLASS - 1) * D_SIDE)], z_send.at[8 + side])
        await_bytes(hd.at[pl.ds(0, CLASS * D_SIDE)], z_send.at[10 + side])
    await_bytes(fin_slots.at[pl.ds(0, RINGS - 1)], z_send.at[4])
    await_bytes(qall.at[pl.ds(0, 3)], q_send.at[0])
    await_bytes(xd.at[pl.ds(0, 10 * piece_rows // 2)], q_send.at[1])


def shards(
    example_token_inputs,
    example_token_cotangents,
    query_token_inputs,
    query_token_cotangents,
    example_token_lengths,
    query_token_lengths,
    adapter_down_snapshots,
    adapter_up_snapshots,
    down_first_moment,
    down_second_moment,
    up_first_moment,
    up_second_moment,
    snapshot_learning_rates,
):
    anywhere, scalars = pl.BlockSpec(memory_space=pl.ANY), pl.BlockSpec(memory_space=pltpu.SMEM)
    vmem = pltpu.VMEM
    dma = pltpu.SemaphoreType.DMA
    return pl.pallas_call(
        kernel,
        out_shape=jax.ShapeDtypeStruct((DEMOS, EX * QUERIES), F32),
        in_specs=[anywhere] * 10 + [scalars] * 3,
        out_specs=pl.BlockSpec(memory_space=vmem),
        scratch_shapes=[
            vmem((QUERIES * TOKENS, FEATURES), BF16),
            vmem((QUERIES * TOKENS, FEATURES), BF16),
            vmem((DEMOS * TOKENS, FEATURES), BF16),
            vmem((DEMOS * TOKENS, FEATURES), BF16),
            vmem((RANKS, FEATURES), BF16),
            vmem((RANKS, FEATURES), BF16),
            vmem((RANKS, FEATURES), F32),
            vmem((RANKS, FEATURES), F32),
            vmem((RANKS, FEATURES), F32),
            vmem((RANKS, FEATURES), F32),
            vmem((PAIR, FEATURES), F32),
            vmem((PAIR, FEATURES), F32),
            vmem((QUERIES * PAIR, TOKENS), F32),
            vmem((Q_HALF, TOKENS), F32),
            vmem((DEMOS * PAIR, TOKENS), F32),
            vmem((D_HALF, TOKENS), F32),
            vmem((Q_HALF, TOKENS), BF16),
            vmem((2, RINGS, Q_UNIT, TOKENS), BF16),
            vmem((D_CLASS, TOKENS), BF16),
            vmem((D_CLASS, TOKENS), BF16),
            vmem((D_CLASS, TOKENS), BF16),
            vmem((2, CLASS, D_SIDE, TOKENS), BF16),
            vmem((QUERIES * PAIR, TOKENS), BF16),
            vmem((DEMOS * PAIR, TOKENS), BF16),
            vmem((2, PAIR * QUERIES, LANES), F32),
            vmem((2, PAIR * DEMOS, LANES), F32),
            vmem((EX, 4, RANKS * QUERIES, LANES), BF16),
            vmem((LANES, LANES), F32),
            vmem((3, QUERIES * TOKENS, FEATURES), BF16),
            vmem((3, QUERIES * RANKS, TOKENS), BF16),
            vmem((8, LANES), F32),
            vmem((8, LANES), F32),
            vmem((8, LANES), F32),
            vmem((RINGS, 8, LANES), F32),
            vmem((2, 8, LANES), F32),
            vmem((3, 8, LANES), F32),
            dma((10,)),
            dma((8,)),
            dma((8,)),
            dma((12,)),
            dma((12,)),
            dma((2,)),
            dma((EX, 4)),
            dma((3, 3)),
            dma((3, 3)),
            dma((3,)),
            dma((3,)),
        ],
        compiler_params=pltpu.CompilerParams(collective_id=0, has_side_effects=True, vmem_limit_bytes=60 * 2**20),
    )(
        query_token_inputs.reshape(QUERIES * TOKENS, FEATURES),
        query_token_cotangents.reshape(QUERIES * TOKENS, FEATURES),
        example_token_inputs.reshape(DEMOS * TOKENS, FEATURES),
        example_token_cotangents.reshape(DEMOS * TOKENS, FEATURES),
        adapter_down_snapshots[0].T,
        adapter_up_snapshots[0],
        down_first_moment[0].T,
        down_second_moment[0].T,
        up_first_moment[0],
        up_second_moment[0],
        query_token_lengths,
        example_token_lengths,
        snapshot_learning_rates,
    )


def solution(mesh):
    in_specs = (
        P("ckpt", "ex", None, "par"),
        P("ckpt", "ex", None, "par"),
        P("ckpt", "ex", None, "par"),
        P("ckpt", "ex", None, "par"),
        P("ex"),
        P("ex"),
        P("ckpt", "par", None),
        P("ckpt", None, "par"),
        P("ckpt", "par", None),
        P("ckpt", "par", None),
        P("ckpt", None, "par"),
        P("ckpt", None, "par"),
        P("ckpt"),
    )
    out_specs = P("ex", None)
    return jax.shard_map(shards, mesh=mesh, in_specs=in_specs, out_specs=out_specs, check_vma=False)
```
